128 devices in a mesh: group: 4 (over z_lo, core), expert: 32 (over x, y, z_hi).
Axes of the slice: x: 4, y: 4, z: 4 (z_hi: 2, z_lo: 2; z = z_hi * 2 + z_lo), core: 2. Of those that a mesh axis runs over, the one named last changes fastest.
Arguments:
- images: bfloat16 [512, 256, 1280], P(('group', 'expert')), may hold values from -6 to 6
- dispatch_weight: bfloat16 [1280, 64], replicated, may hold values from -6 to 6
- weight_in: bfloat16 [64, 1280, 2560], P('expert', None, 'group'), may hold values from -0.15625 to 0.15625
- weight_out: bfloat16 [64, 2560, 1280], P('expert', 'group'), may hold values from -0.125 to 0.125
- out_grad: bfloat16 [512, 256, 1280], P(('group', 'expert')), may hold values from -6 to 6
Outputs:
- mixed: bfloat16 [512, 256, 1280], P(('group', 'expert'))
- grad_images: bfloat16 [512, 256, 1280], P(('group', 'expert'))
- grad_dispatch: float32 [1280, 64], replicated
- grad_w_in: bfloat16 [64, 1280, 2560], P('expert', None, 'group')
- grad_w_out: bfloat16 [64, 2560, 1280], P('expert', 'group')
The draws below stay inside these ranges and needn't reach their ends.
All inputs are finite; a program needn't handle non-finite values.
Results may differ from the reference program's by a relative error of at most 0.017.
Values may be sent and summed in bfloat16 or wider, within the bound.
A program may use at most 128 MiB of HBM per device.

```python
import math
import jax
import jax.numpy as jnp
from jax import lax

D = 1280
EXPERTS = 64
HID = 2560
TOK = 256
IMAGES = 512


def draw_images(key, part):
    key = jax.random.fold_in(key, 11)
    values = jnp.clip(jax.random.normal(key, (IMAGES, TOK, D), jnp.float32), -6.0, 6.0)
    return values.astype(jnp.bfloat16)


def draw_dispatch_weight(key, part):
    key = jax.random.fold_in(key, 23)
    spread = 3.0 / math.sqrt(D)
    values = jnp.clip(jax.random.normal(key, (D, EXPERTS), jnp.float32) * spread, -3.0, 3.0)
    return values.astype(jnp.bfloat16)


def level_of(own_key, extent, split, smallest, high):
    def one(dim, shards_of):
        heights = jax.random.uniform(jax.random.fold_in(jax.random.fold_in(own_key, 6), dim), (shards_of,), jnp.float32, smallest / len(split), high / len(split))
        return jnp.repeat(jnp.exp(heights), extent[dim] // shards_of).reshape((-1,) + (1,) * (len(extent) - dim - 1))

    gain = one(*split[0])
    for cut in split[1:]:
        gain = gain * one(*cut)
    return gain


def centred(own_key, shape, deviation, most, shards=(), kind=jnp.bfloat16):
    array = jax.random.normal(own_key, shape, jnp.float32) * deviation
    if len(shards) > 0:
        array = level_of(own_key, shape, shards, -0.22, 0.18) * array
    return jnp.clip(array, min=-most, max=most).astype(kind)


def setup_inputs(seed: int = 0) -> dict:
    splits = jax.random.split(jax.random.key(seed), 6)
    images = draw_images(jax.random.fold_in(splits[5], 71), 0)
    dispatch_weight = draw_dispatch_weight(jax.random.fold_in(splits[5], 71), 0)
    weight_in = centred(splits[2], (EXPERTS, D, HID), D ** -0.5, 0.15625, ((0, 32), (2, 4)))
    weight_out = centred(splits[3], (EXPERTS, HID, D), HID ** -0.5, 0.125, ((0, 32), (1, 4)))
    out_grad = centred(splits[4], (IMAGES, TOK, D), 1.0, 6.0, ((0, 128),))
    return {"images": images, "dispatch_weight": dispatch_weight, "weight_in": weight_in, "weight_out": weight_out, "out_grad": out_grad}


def gelu_pair(hidden_pre):
    normal_cdf = 0.5 * (1.0 + jax.scipy.special.erf(hidden_pre * 0.7071067811865476))
    density = jnp.exp(-0.5 * hidden_pre * hidden_pre) * 0.3989422804014327
    return hidden_pre * normal_cdf, normal_cdf + hidden_pre * density


def reference(images, dispatch_weight, weight_in, weight_out, out_grad):
    def routing(one_image):
        logits = jnp.dot(one_image, dispatch_weight, preferred_element_type=jnp.float32)
        dispatch = jax.nn.softmax(logits, axis=0)
        combine = jax.nn.softmax(logits, axis=1)
        slot_rows = jnp.dot(dispatch.astype(jnp.bfloat16).T, one_image, preferred_element_type=jnp.float32).astype(jnp.bfloat16)
        return slot_rows, dispatch, combine

    slot_rows, dispatch, combine = lax.map(routing, images)
    expert_rows = jnp.swapaxes(slot_rows, 0, 1)

    def expert_forward(inputs):
        rows_here, first, second = inputs
        hidden_pre = jnp.dot(rows_here, first, preferred_element_type=jnp.float32)
        gelu_value, gelu_slope = gelu_pair(hidden_pre)
        hidden_act = gelu_value.astype(jnp.bfloat16)
        return jnp.dot(hidden_act, second, preferred_element_type=jnp.float32).astype(jnp.bfloat16)

    expert_out = jnp.swapaxes(lax.map(expert_forward, (expert_rows, weight_in, weight_out)), 0, 1)

    def combine_step(inputs):
        combine_here, results, cotangent = inputs
        combine_low = combine_here.astype(jnp.bfloat16)
        mixed_here = jnp.dot(combine_low, results, preferred_element_type=jnp.float32).astype(jnp.bfloat16)
        grad_here = jnp.dot(combine_low.T, cotangent, preferred_element_type=jnp.float32).astype(jnp.bfloat16)
        return mixed_here, grad_here

    mixed, expert_grad = lax.map(combine_step, (combine, expert_out, out_grad))

    def expert_backward(inputs):
        rows_here, first, second, grad_here = inputs
        hidden_pre = jnp.dot(rows_here, first, preferred_element_type=jnp.float32)
        gelu_value, gelu_slope = gelu_pair(hidden_pre)
        hidden_act = gelu_value.astype(jnp.bfloat16)
        act_grad = jnp.dot(grad_here, second.T, preferred_element_type=jnp.float32)
        pre_grad = (act_grad * gelu_slope).astype(jnp.bfloat16)
        second_grad = jnp.dot(hidden_act.T, grad_here, preferred_element_type=jnp.float32).astype(jnp.bfloat16)
        first_grad = jnp.dot(rows_here.T, pre_grad, preferred_element_type=jnp.float32).astype(jnp.bfloat16)
        rows_grad = jnp.dot(pre_grad, first.T, preferred_element_type=jnp.float32).astype(jnp.bfloat16)
        return rows_grad, first_grad, second_grad

    rows_grad, grad_w_in, grad_w_out = lax.map(expert_backward, (expert_rows, weight_in, weight_out, jnp.swapaxes(expert_grad, 0, 1)))
    slot_grad = jnp.swapaxes(rows_grad, 0, 1)

    def backward_step(running, inputs):
        one_image, dispatch_here, combine_here, results, cotangent, slot_here = inputs
        dcombine = jnp.dot(cotangent, results.T, preferred_element_type=jnp.float32)
        combine_term = combine_here * (dcombine - jnp.sum(combine_here * dcombine, axis=1, keepdims=True))
        ddispatch = jnp.dot(one_image, slot_here.T, preferred_element_type=jnp.float32)
        dispatch_term = dispatch_here * (ddispatch - jnp.sum(dispatch_here * ddispatch, axis=0, keepdims=True))
        logit_grad = (combine_term + dispatch_term).astype(jnp.bfloat16)
        image_grad = (jnp.dot(logit_grad, dispatch_weight.T, preferred_element_type=jnp.float32)
                      + jnp.dot(dispatch_here.astype(jnp.bfloat16), slot_here, preferred_element_type=jnp.float32)).astype(jnp.bfloat16)
        return running + jnp.dot(one_image.T, logit_grad, preferred_element_type=jnp.float32), image_grad

    grad_dispatch, grad_images = lax.scan(backward_step, jnp.zeros((D, EXPERTS), jnp.float32),
                                          (images, dispatch, combine, expert_out, out_grad, slot_grad))
    return mixed, grad_images, grad_dispatch, grad_w_in, grad_w_out
```

```python
import functools

import jax
import jax.numpy as jnp
from jax import lax
from jax.experimental import pallas as pl
from jax.experimental.pallas import tpu as pltpu
from jax.sharding import PartitionSpec as P

MESH = pl.DeviceIdType.MESH
F32, BF16 = jnp.float32, jnp.bfloat16

D, HIDQ, TOK, IMG, EXP = 1280, 640, 256, 4, 64
ROWS = EXP * IMG
T = IMG * TOK
HALF = D // 2
N = 32
NT = (((1,), (1,)), ((), ()))
TN = (((0,), (0,)), ((), ()))


def dot(a, b, dims=(((1,), (0,)), ((), ()))):
    return lax.dot_general(a, b, dims, preferred_element_type=F32)


def gelu_pair(v):
    cdf = 0.5 * (1.0 + lax.erf(v * 0.7071067811865476))
    density = jnp.exp(-0.5 * v * v) * 0.3989422804014327
    return v * cdf, cdf + v * density


def pack_rows(rows):
    n = rows.shape[0] // 8
    left = rows[:, :HALF].reshape(n, 8, HALF)
    right = rows[:, HALF:].reshape(n, 8, HALF)
    return jnp.concatenate([left, right], axis=1).astype(BF16)


def unpack_rows(messages):
    n = messages.shape[0]
    left = messages[:, :8].reshape(8 * n, HALF)
    right = messages[:, 8:].reshape(8 * n, HALF)
    return jnp.concatenate([left, right], axis=1)


def low_rows(shape):
    return lax.broadcasted_iota(jnp.int32, shape, 1) < 4


def split_experts(messages):
    n = messages.shape[0] // 2
    parts = [[], []]
    for half in range(2):
        block = messages[:, 8 * half : 8 * half + 8].reshape(n, 2, 8, HALF)
        a, b = block[:, 0], block[:, 1]
        low = low_rows(a.shape)
        parts[0].append(jnp.where(low, a, pltpu.roll(b, 4, 1)).reshape(8 * n, HALF))
        parts[1].append(jnp.where(low, pltpu.roll(a, 4, 1), b).reshape(8 * n, HALF))
    return [jnp.concatenate(p, axis=1).astype(BF16) for p in parts]


def join_experts(first, second):
    n = first.shape[0] // 8
    halves = []
    for half in range(2):
        p0 = first[:, HALF * half : HALF * (half + 1)].reshape(n, 8, HALF)
        p1 = second[:, HALF * half : HALF * (half + 1)].reshape(n, 8, HALF)
        low = low_rows(p0.shape)
        a = jnp.where(low, p0, pltpu.roll(p1, 4, 1))
        b = jnp.where(low, pltpu.roll(p0, 4, 1), p1)
        halves.append(jnp.stack([a, b], axis=1).reshape(2 * n, 8, HALF))
    return jnp.concatenate(halves, axis=1).astype(BF16)


def kernel(
    x_hbm, wd_hbm, win_hbm, wout_hbm, g_hbm,
    mixed_hbm, gimg_hbm, gd_hbm, gwin_hbm, gwout_hbm,
    x, wd, win, wout, g, wrep, send1, send2, r1, r2, e1, e2, act, slope, pre,
    p1, p2, pc1, pc2, ret1, ret2, dis, com, dis_low, com_low, lgrad, eo, sg,
    mixed, gimg, gwin, gwout, gd, ar_a, ar_x, ar_y, gdo,
    in_sem, out_sem, ssem, d_sem, c_sem, b_sem, ret_sem, ar_sem,
):
    group, me = lax.axis_index("group"), lax.axis_index("expert")
    zlo, core = group // 2, group % 2
    xx, yy, zhi = me // 8, (me // 2) % 4, me % 2

    def far(dz, r):
        dx, dy, dh = r // 8, (r // 2) % 4, r % 2
        e = (((xx + dx) % 4) * 4 + (yy + dy) % 4) * 2 + (zhi + dh) % 2
        return (zlo + dz) % 2, e

    def near(k):
        dz, dc, dh = k // 4, (k // 2) % 2, k % 2
        zl, c, zh = (zlo + dz) % 2, (core + dc) % 2, (zhi + dh) % 2
        return zl, c, zh, (zh * 2 + zl) * 2 + c

    def remote(src, dst, send, recv, device):
        return pltpu.make_async_remote_copy(
            src_ref=src, dst_ref=dst, send_sem=send, recv_sem=recv, device_id=device, device_id_type=MESH
        )

    def arrived(ref, sem):
        pltpu.make_async_copy(ref, ref, sem).wait()

    partner = (zlo * 2 + 1 - core, me)

    loads = [
        pltpu.make_async_copy(src, dst, in_sem.at[k])
        for k, (src, dst) in enumerate(((wd_hbm, wd), (x_hbm, x), (g_hbm, g), (win_hbm, win), (wout_hbm, wout)))
    ]
    for load in loads:
        load.start()

    barrier = pltpu.get_barrier_semaphore()

    def greet(k, _):
        zl, e = far(k // N, k % N)
        pl.semaphore_signal(barrier, inc=1, device_id=(zl * 2 + core, e), device_id_type=MESH)
        return 0

    lax.fori_loop(1, 2 * N, greet, 0)
    pl.semaphore_signal(barrier, inc=1, device_id=partner, device_id_type=MESH)
    for dz, dh in ((0, 1), (1, 0), (1, 1)):
        e = (xx * 4 + yy) * 2 + (zhi + dh) % 2
        pl.semaphore_signal(
            barrier, inc=1, device_id=(((zlo + dz) % 2) * 2 + 1 - core, e), device_id_type=MESH
        )

    loads[0].wait()
    rep = (
        lax.broadcasted_iota(jnp.int32, (ROWS, EXP), 0) // IMG
        == lax.broadcasted_iota(jnp.int32, (ROWS, EXP), 1)
    )
    wrep[...] = dot(rep.astype(F32).astype(BF16), wd[...], NT).astype(BF16)
    loads[1].wait()

    def route(i, _):
        cols = pl.ds(pl.multiple_of(i * TOK, TOK), TOK)
        logits = dot(wrep[...], x[cols, :], NT)
        own = lax.broadcasted_iota(jnp.int32, (ROWS, TOK), 0) % IMG == i
        up = jnp.exp(logits - jnp.max(logits, axis=1, keepdims=True))
        d = jnp.where(own, up / jnp.sum(up, axis=1, keepdims=True), 0.0)
        dis[:, cols] = d
        dis_low[:, cols] = d.astype(BF16)
        up = jnp.where(own, jnp.exp(logits - jnp.max(logits, axis=0, keepdims=True)), 0.0)
        c = up / jnp.sum(up, axis=0, keepdims=True)
        com[:, cols] = c
        com_low[:, cols] = c.astype(BF16)
        return 0

    lax.fori_loop(0, IMG, route, 0)
    send1[...] = pack_rows(dot(dis_low[...], x[...]))
    pl.semaphore_wait(barrier, 2 * N - 1 + 4)

    def dispatch(send, rows, which):
        def one(k, _):
            zl, e = far(k // N, k % N)
            remote(
                send.at[e], rows.at[core * 2 * N + zlo * N + me], ssem.at[which], d_sem.at[which, zlo],
                (zl * 2 + core, e),
            ).start()
            return 0

        pltpu.make_async_copy(send.at[me], rows.at[core * 2 * N + zlo * N + me], d_sem.at[which, zlo]).start()
        lax.fori_loop(1, 2 * N, one, 0)

    dispatch(send1, r1, 0)
    loads[2].wait()
    send2[...] = pack_rows(dot(com_low[...], g[...]))
    dispatch(send2, r2, 1)

    def quarter(c, dz):
        return pl.ds(c * 2 * N + ((zlo + dz) % 2) * N, N)

    def share(rows, which):
        for dz in range(2):
            block = rows.at[quarter(core, dz)]
            arrived(block, d_sem.at[which, (zlo + dz) % 2])
            remote(block, block, ssem.at[2 + which], c_sem.at[which, dz], partner).start()

    def per_expert(rows, out, c, dz, at):
        base = c * 2 * N + ((zlo + dz) % 2) * N

        def step(s, _):
            first, second = split_experts(rows[pl.ds(base + s * 8, 8)].astype(F32))
            to = pl.ds(pl.multiple_of(at * 4 * N + s * 32, 32), 32)
            out[0, to, :] = first
            out[1, to, :] = second
            return 0

        lax.fori_loop(0, N // 8, step, 0)

    def forward(c, dz, at):
        per_expert(r1, e1, c, dz, at)
        to = pl.ds(pl.multiple_of(at * 4 * N, 4 * N), 4 * N)
        partial = []
        for ex in range(2):
            value, grad = gelu_pair(dot(e1[ex, to, :], win[ex]))
            slope[ex, to, :] = grad
            low = value.astype(BF16)
            act[ex, to, :] = low
            partial.append(dot(low, wout[ex]))
        p1[quarter(c, dz)] = join_experts(*partial)

    def backward(c, dz, at):
        per_expert(r2, e2, c, dz, at)
        to = pl.ds(pl.multiple_of(at * 4 * N, 4 * N), 4 * N)
        partial = []
        for ex in range(2):
            low = (dot(e2[ex, to, :], wout[ex], NT) * slope[ex, to, :]).astype(BF16)
            pre[ex, to, :] = low
            partial.append(dot(low, win[ex], NT))
        p2[quarter(c, dz)] = join_experts(*partial)

    def experts(step, rows, p, pc, which):
        def own(dz, _):
            step(core, dz, dz)
            return 0

        def other(dz, _):
            arrived(rows.at[quarter(1 - core, dz)], c_sem.at[which, dz])
            step(1 - core, dz, 2 + dz)
            remote(
                p.at[quarter(1 - core, dz)], pc.at[pl.ds(dz * N, N)], ssem.at[4 + which], b_sem.at[which, dz], partner
            ).start()
            return 0

        lax.fori_loop(0, 2, own, 0)
        lax.fori_loop(0, 2, other, 0)

    def give_back(p, pc, ret, which):
        for dz in range(2):
            arrived(pc.at[pl.ds(dz * N, N)], b_sem.at[which, dz])
            zl = (zlo + dz) % 2
            base = core * 2 * N + zl * N

            def add(s, _):
                at = pl.ds(base + s * 8, 8)
                p[at] = (p[at].astype(F32) + pc[pl.ds(dz * N + s * 8, 8)].astype(F32)).astype(BF16)
                return 0

            lax.fori_loop(0, N // 8, add, 0)
            to = ret.at[zlo * N + me]

            def one(r, _):
                _, e = far(dz, r)
                remote(p.at[base + e], to, ssem.at[6 + which], ret_sem.at[which], (zl * 2 + core, e)).start()
                return 0

            if dz == 0:
                pltpu.make_async_copy(p.at[base + me], to, ret_sem.at[which]).start()
            lax.fori_loop(1 - dz, N, one, 0)

    loads[3].wait()
    loads[4].wait()
    share(r1, 0)
    experts(forward, r1, p1, pc1, 0)
    give_back(p1, pc1, ret1, 0)
    share(r2, 1)
    experts(backward, r2, p2, pc2, 1)
    give_back(p2, pc2, ret2, 1)

    def weight_grads(m, _):
        cut = pl.ds(pl.multiple_of(m * 128, 128), 128)
        wide = pl.ds(pl.multiple_of(m * 256, 256), 256)
        for ex in range(2):
            gwout[ex, cut, :] = dot(act[ex, :, cut], e2[ex], TN).astype(BF16)
            gwin[ex, wide, :] = dot(e1[ex, :, wide], pre[ex], TN).astype(BF16)
        return 0

    lax.fori_loop(0, 5, weight_grads, 0)
    out_gwin = pltpu.make_async_copy(gwin, gwin_hbm, out_sem.at[0])
    out_gwout = pltpu.make_async_copy(gwout, gwout_hbm, out_sem.at[1])
    out_gwin.start()
    out_gwout.start()

    def returned(ret, which):
        arrived(ret, ret_sem.at[which])
        return unpack_rows(ret[pl.ds(0, N)].astype(F32) + ret[pl.ds(N, N)].astype(F32)).astype(BF16)

    eo[...] = returned(ret1, 0)

    def mix(i, _):
        cols = pl.ds(pl.multiple_of(i * TOK, TOK), TOK)
        mixed[cols, :] = dot(com_low[:, cols], eo[...], TN).astype(BF16)
        c = com[:, cols]
        dc = dot(eo[...], g[cols, :], NT)
        com[:, cols] = c * (dc - jnp.sum(c * dc, axis=0, keepdims=True))
        return 0

    lax.fori_loop(0, IMG, mix, 0)
    out_mixed = pltpu.make_async_copy(mixed, mixed_hbm, out_sem.at[2])
    out_mixed.start()

    sg[...] = returned(ret2, 1)
    pick = (
        lax.broadcasted_iota(jnp.int32, (EXP, ROWS), 1) // IMG
        == lax.broadcasted_iota(jnp.int32, (EXP, ROWS), 0)
    ).astype(F32).astype(BF16)
    gd[...] = jnp.zeros_like(gd)

    def logit_grads(i, _):
        cols = pl.ds(pl.multiple_of(i * TOK, TOK), TOK)
        d = dis[:, cols]
        dd = dot(sg[...], x[cols, :], NT)
        low = (com[:, cols] + d * (dd - jnp.sum(d * dd, axis=1, keepdims=True))).astype(BF16)
        lgrad[:, cols] = low
        gd[...] += dot(dot(pick, low).astype(BF16), x[cols, :])
        return 0

    lax.fori_loop(0, IMG, logit_grads, 0)

    block = (zhi * 2 + zlo) * 2 + core

    def rows8(b):
        return pl.ds(pl.multiple_of(b * 8, 8), 8)

    def near_device(k):
        zl, c, zh, b = near(k)
        return (zl * 2 + c, (xx * 4 + yy) * 2 + zh), b

    for k in range(1, 8):
        device, b = near_device(k)
        remote(gd.at[rows8(b)], ar_a.at[k], ssem.at[8], ar_sem.at[0], device).start()

    def image_grad(i):
        cols = pl.ds(i * TOK, TOK)
        gimg[cols, :] = (dot(lgrad[:, cols], wrep[...], TN) + dot(dis_low[:, cols], sg[...], TN)).astype(BF16)
        copy = pltpu.make_async_copy(gimg.at[cols], gimg_hbm.at[cols], out_sem.at[3 + i])
        copy.start()
        return copy

    outs = [image_grad(0)]
    arrived(ar_a.at[pl.ds(1, 7)], ar_sem.at[0])
    total = gd[rows8(block), :]
    for k in range(1, 8):
        total += ar_a[k]
    ar_x[xx] = total
    for k in range(1, 4):
        remote(
            ar_x.at[xx], ar_x.at[xx], ssem.at[9], ar_sem.at[1], (group, (((xx + k) % 4) * 4 + yy) * 2 + zhi)
        ).start()
    outs.append(image_grad(1))
    arrived(ar_x.at[pl.ds(0, 3)], ar_sem.at[1])
    ar_y[yy] = (ar_x[0] + ar_x[1]) + (ar_x[2] + ar_x[3])
    for k in range(1, 4):
        remote(
            ar_y.at[yy], ar_y.at[yy], ssem.at[10], ar_sem.at[2], (group, (xx * 4 + (yy + k) % 4) * 2 + zhi)
        ).start()
    outs.append(image_grad(2))
    arrived(ar_y.at[pl.ds(0, 3)], ar_sem.at[2])
    gdo[rows8(block), :] = (ar_y[0] + ar_y[1]) + (ar_y[2] + ar_y[3])
    for k in range(1, 8):
        device, _ = near_device(k)
        remote(gdo.at[rows8(block)], gdo.at[rows8(block)], ssem.at[11], ar_sem.at[3], device).start()
    outs.append(image_grad(3))
    arrived(gdo.at[pl.ds(0, 56)], ar_sem.at[3])
    out_gd = pltpu.make_async_copy(gdo, gd_hbm, out_sem.at[7])
    out_gd.start()

    for which in range(2):
        arrived(r1.at[pl.ds(0, 2 * N - 1)], ssem.at[which])
        arrived(r1.at[pl.ds(0, 2 * N)], ssem.at[2 + which])
        arrived(r1.at[pl.ds(0, 2 * N)], ssem.at[4 + which])
        arrived(r1.at[pl.ds(0, 2 * N - 1)], ssem.at[6 + which])
    arrived(gd.at[pl.ds(0, 56)], ssem.at[8])
    arrived(ar_x.at[pl.ds(0, 3)], ssem.at[9])
    arrived(ar_y.at[pl.ds(0, 3)], ssem.at[10])
    arrived(gd.at[pl.ds(0, 56)], ssem.at[11])
    for copy in [out_gwin, out_gwout, out_mixed, *outs, out_gd]:
        copy.wait()


def per_device(images, dispatch_weight, weight_in, weight_out, out_grad):
    vmem = pltpu.VMEM
    message = (16, HALF)
    scratch = [
        vmem((T, D), BF16), vmem((D, EXP), BF16), vmem((2, D, HIDQ), BF16), vmem((2, HIDQ, D), BF16), vmem((T, D), BF16),
        vmem((ROWS, D), BF16),
        vmem((N, *message), BF16), vmem((N, *message), BF16),
        vmem((4 * N, *message), BF16), vmem((4 * N, *message), BF16),
        vmem((2, 16 * N, D), BF16), vmem((2, 16 * N, D), BF16),
        vmem((2, 16 * N, HIDQ), BF16), vmem((2, 16 * N, HIDQ), F32), vmem((2, 16 * N, HIDQ), BF16),
        vmem((4 * N, *message), BF16), vmem((4 * N, *message), BF16),
        vmem((2 * N, *message), BF16), vmem((2 * N, *message), BF16),
        vmem((2 * N, *message), BF16), vmem((2 * N, *message), BF16),
        vmem((ROWS, T), F32), vmem((ROWS, T), F32), vmem((ROWS, T), BF16), vmem((ROWS, T), BF16), vmem((ROWS, T), BF16),
        vmem((ROWS, D), BF16), vmem((ROWS, D), BF16),
        vmem((T, D), BF16), vmem((T, D), BF16), vmem((2, D, HIDQ), BF16), vmem((2, HIDQ, D), BF16),
        vmem((EXP, D), F32), vmem((8, 8, D), F32), vmem((4, 8, D), F32), vmem((4, 8, D), F32), vmem((EXP, D), F32),
        pltpu.SemaphoreType.DMA((5,)), pltpu.SemaphoreType.DMA((8,)), pltpu.SemaphoreType.DMA((12,)),
        pltpu.SemaphoreType.DMA((2, 2)), pltpu.SemaphoreType.DMA((2, 2)), pltpu.SemaphoreType.DMA((2, 2)),
        pltpu.SemaphoreType.DMA((2,)), pltpu.SemaphoreType.DMA((4,)),
    ]
    anywhere = pl.BlockSpec(memory_space=pl.ANY)
    mixed, gimg, gd, gwin, gwout = pl.pallas_call(
        kernel,
        out_shape=(
            jax.ShapeDtypeStruct((T, D), BF16),
            jax.ShapeDtypeStruct((T, D), BF16),
            jax.ShapeDtypeStruct((EXP, D), F32),
            jax.ShapeDtypeStruct((2, D, HIDQ), BF16),
            jax.ShapeDtypeStruct((2, HIDQ, D), BF16),
        ),
        in_specs=[anywhere] * 5,
        out_specs=[anywhere] * 5,
        scratch_shapes=scratch,
        compiler_params=pltpu.CompilerParams(
            collective_id=0, has_side_effects=True, vmem_limit_bytes=62 * 2**20
        ),
    )(images.reshape(T, D), dispatch_weight, weight_in, weight_out, out_grad.reshape(T, D))
    return mixed.reshape(IMG, TOK, D), gimg.reshape(IMG, TOK, D), gd.T, gwin, gwout


def solution(mesh):
    tokens = P(("group", "expert"), None, None)
    first, second = P("expert", None, "group"), P("expert", "group", None)
    return jax.shard_map(
        per_device,
        mesh=mesh,
        in_specs=(tokens, P(), first, second, tokens),
        out_specs=(tokens, tokens, P(), first, second),
        check_vma=False,
    )
```

```python
import jax
import jax.numpy as jnp
from jax import lax
from jax.experimental import pallas as pl
from jax.experimental.pallas import tpu as pltpu
from jax.sharding import PartitionSpec as P

MESH = pl.DeviceIdType.MESH
LIMIT = 42
F32, BF16 = jnp.float32, jnp.bfloat16

D, HIDQ, TOK, IMG, EXP = 1280, 640, 256, 4, 64
ROWS = EXP * IMG
T = IMG * TOK
HALF = D // 2
N = 32
NT = (((1,), (1,)), ((), ()))
TN = (((0,), (0,)), ((), ()))


def dot(a, b, dims=(((1,), (0,)), ((), ()))):
    return lax.dot_general(a, b, dims, preferred_element_type=F32)


def gelu_pair(v):
    cdf = 0.5 * (1.0 + lax.erf(v * 0.7071067811865476))
    density = jnp.exp(-0.5 * v * v) * 0.3989422804014327
    return v * cdf, cdf + v * density


def pack_rows(rows):
    n = rows.shape[0] // 8
    left = rows[:, :HALF].reshape(n, 8, HALF)
    right = rows[:, HALF:].reshape(n, 8, HALF)
    return jnp.concatenate([left, right], axis=1).astype(BF16)


def unpack_rows(messages):
    n = messages.shape[0]
    left = messages[:, :8].reshape(8 * n, HALF)
    right = messages[:, 8:].reshape(8 * n, HALF)
    return jnp.concatenate([left, right], axis=1)


def low_rows(shape):
    return lax.broadcasted_iota(jnp.int32, shape, 1) < 4


def split_experts(messages):
    n = messages.shape[0] // 2
    parts = [[], []]
    for half in range(2):
        block = messages[:, 8 * half : 8 * half + 8].reshape(n, 2, 8, HALF)
        a, b = block[:, 0], block[:, 1]
        low = low_rows(a.shape)
        parts[0].append(jnp.where(low, a, pltpu.roll(b, 4, 1)).reshape(8 * n, HALF))
        parts[1].append(jnp.where(low, pltpu.roll(a, 4, 1), b).reshape(8 * n, HALF))
    return [jnp.concatenate(p, axis=1).astype(BF16) for p in parts]


def join_experts(first, second):
    n = first.shape[0] // 8
    halves = []
    for half in range(2):
        p0 = first[:, HALF * half : HALF * (half + 1)].reshape(n, 8, HALF)
        p1 = second[:, HALF * half : HALF * (half + 1)].reshape(n, 8, HALF)
        low = low_rows(p0.shape)
        a = jnp.where(low, p0, pltpu.roll(p1, 4, 1))
        b = jnp.where(low, pltpu.roll(p0, 4, 1), p1)
        halves.append(jnp.stack([a, b], axis=1).reshape(2 * n, 8, HALF))
    return jnp.concatenate(halves, axis=1).astype(BF16)


def kernel(
    x_hbm, wd_hbm, win_hbm, wout_hbm, g_hbm,
    mix0, mix1, mix2, mix3, grad0, grad1, grad2, grad3, win0, win1, win2, win3, win4, wout0, wout1, wout2, wout3, wout4,
    gd_out,
    x, wd, win, wout, g, send1, send2, r1, r2, e1, e2, act, slope, pre,
    p1, pc, ret1, ret2, dis, com, dis_low, com_low, spread_low, lgrad, eo, sg,
    gwin, gd, ar_a, ar_x, ar_y, gdo,
    in_sem, out_sem, w_sem, ssem, d_sem, c_sem, b_sem, ret_sem, ar_sem,
):
    group, me = lax.axis_index("group"), lax.axis_index("expert")
    zlo, core = group // 2, group % 2
    xx, yy, zhi = me // 8, (me // 2) % 4, me % 2

    def far(dz, r):
        dx, dy, dh = r // 8, (r // 2) % 4, r % 2
        e = (((xx + dx) % 4) * 4 + (yy + dy) % 4) * 2 + (zhi + dh) % 2
        return (zlo + dz) % 2, e

    def near(k):
        dz, dc, dh = k // 4, (k // 2) % 2, k % 2
        zl, c, zh = (zlo + dz) % 2, (core + dc) % 2, (zhi + dh) % 2
        return zl, c, zh, (zh * 2 + zl) * 2 + c

    def remote(src, dst, send, recv, device):
        return pltpu.make_async_remote_copy(
            src_ref=src, dst_ref=dst, send_sem=send, recv_sem=recv, device_id=device, device_id_type=MESH
        )

    def arrived(ref, sem):
        pltpu.make_async_copy(ref, ref, sem).wait()

    partner = (zlo * 2 + 1 - core, me)

    loads = [
        pltpu.make_async_copy(src, dst, in_sem.at[k])
        for k, (src, dst) in enumerate(((wd_hbm, wd), (x_hbm, x), (g_hbm, g), (win_hbm, win), (wout_hbm, wout)))
    ]
    loads[0].start()
    loads[1].start()

    barrier = pltpu.get_barrier_semaphore()

    def greet(k, _):
        zl, e = far(k // N, k % N)
        pl.semaphore_signal(barrier, inc=1, device_id=(zl * 2 + core, e), device_id_type=MESH)
        return 0

    lax.fori_loop(1, 2 * N, greet, 0)
    pl.semaphore_signal(barrier, inc=1, device_id=partner, device_id_type=MESH)
    for dz, dh in ((0, 1), (1, 0), (1, 1)):
        e = (xx * 4 + yy) * 2 + (zhi + dh) % 2
        pl.semaphore_signal(
            barrier, inc=1, device_id=(((zlo + dz) % 2) * 2 + 1 - core, e), device_id_type=MESH
        )

    def image(i):
        return pl.ds(i * TOK, TOK)

    def pick(i):
        row = lax.broadcasted_iota(jnp.int32, (EXP, ROWS), 0)
        col = lax.broadcasted_iota(jnp.int32, (EXP, ROWS), 1)
        return jnp.where(col == row * IMG + i, 1.0, 0.0).astype(BF16)

    def spread(low, out):
        for i in range(IMG):
            out[:, image(i)] = dot(pick(i), low[:, image(i)], TN).astype(BF16)

    loads[0].wait()
    loads[1].wait()
    for load in loads[2:]:
        load.start()
    for i in range(IMG):
        scores = dot(wd[...], x[image(i), :], NT)
        com[:, image(i)] = scores
        up = jnp.exp(scores - jnp.max(scores, axis=1, keepdims=True))
        d = up / jnp.sum(up, axis=1, keepdims=True)
        dis[:, image(i)] = d
        dis_low[:, image(i)] = d.astype(BF16)
    spread(dis_low, spread_low)
    send1[...] = pack_rows(dot(spread_low[...], x[...]))
    pl.semaphore_wait(barrier, 2 * N - 1 + 4)

    def dispatch(send, rows, which):
        def one(k, _):
            zl, e = far(k // N, k % N)
            remote(
                send.at[e], rows.at[core * 2 * N + zlo * N + me], ssem.at[which], d_sem.at[which, zlo],
                (zl * 2 + core, e),
            ).start()
            return 0

        pltpu.make_async_copy(send.at[me], rows.at[core * 2 * N + zlo * N + me], d_sem.at[which, zlo]).start()
        lax.fori_loop(1, 2 * N, one, 0)

    dispatch(send1, r1, 0)
    for i in range(IMG):
        scores = com[:, image(i)]
        up = jnp.exp(scores - jnp.max(scores, axis=0, keepdims=True))
        c = up / jnp.sum(up, axis=0, keepdims=True)
        com[:, image(i)] = c
        com_low[:, image(i)] = c.astype(BF16)
    spread(com_low, spread_low)
    loads[2].wait()
    send2[...] = pack_rows(dot(spread_low[...], g[...]))
    dispatch(send2, r2, 1)
    outs = []

    def emit(src, dst, k):
        copy = pltpu.make_async_copy(src, dst, out_sem.at[k])
        copy.start()
        outs.append(copy)


    def quarter(c, dz):
        return pl.ds(c * 2 * N + ((zlo + dz) % 2) * N, N)

    def per_expert(rows, out, c, dz, at):
        base = c * 2 * N + ((zlo + dz) % 2) * N

        def step(s, _):
            first, second = split_experts(rows[pl.ds(base + s * 8, 8)].astype(F32))
            to = pl.ds(pl.multiple_of(at * 4 * N + s * 32, 32), 32)
            out[0, to, :] = first
            out[1, to, :] = second
            return 0

        lax.fori_loop(0, N // 8, step, 0)

    def forward(c, dz, at):
        per_expert(r1, e1, c, dz, at)
        to = pl.ds(pl.multiple_of(at * 4 * N, 4 * N), 4 * N)
        partial = []
        for ex in range(2):
            value, grad = gelu_pair(dot(e1[ex, to, :], win[ex]))
            slope[ex, to, :] = grad.astype(BF16)
            low = value.astype(BF16)
            act[ex, to, :] = low
            partial.append(dot(low, wout[ex]))
        p1[quarter(c, dz)] = join_experts(*partial)

    def backward(c, dz, at):
        per_expert(r2, e2, c, dz, at)
        to = pl.ds(pl.multiple_of(at * 4 * N, 4 * N), 4 * N)
        partial = []
        for ex in range(2):
            low = (dot(e2[ex, to, :], wout[ex], NT) * slope[ex, to, :].astype(F32)).astype(BF16)
            pre[ex, to, :] = low
            partial.append(dot(low, win[ex], NT))
        r1[quarter(c, dz)] = join_experts(*partial)

    def experts(step, rows, p, pc, which):
        def part(dz, _):
            block = rows.at[quarter(core, dz)]
            arrived(block, d_sem.at[which, (zlo + dz) % 2])
            remote(block, block, ssem.at[2 + which], c_sem.at[which, dz], partner).start()
            step(core, dz, 2 * dz)
            theirs = quarter(1 - core, dz)
            arrived(rows.at[theirs], c_sem.at[which, dz])
            step(1 - core, dz, 2 * dz + 1)
            remote(
                p.at[theirs], pc.at[pl.ds(dz * N, N)], ssem.at[4 + which], b_sem.at[which, dz], partner
            ).start()
            return 0

        lax.fori_loop(0, 2, part, 0)

    def give_back(p, pc, ret, which):
        for dz in range(2):
            arrived(pc.at[pl.ds(dz * N, N)], b_sem.at[which, dz])
            zl = (zlo + dz) % 2
            base = core * 2 * N + zl * N

            def add(s, _):
                at = pl.ds(base + s * 8, 8)
                p[at] = (p[at].astype(F32) + pc[pl.ds(dz * N + s * 8, 8)].astype(F32)).astype(BF16)
                return 0

            lax.fori_loop(0, N // 8, add, 0)
            to = ret.at[zlo * N + me]

            def one(r, _):
                _, e = far(dz, r)
                remote(p.at[base + e], to, ssem.at[6 + which], ret_sem.at[which], (zl * 2 + core, e)).start()
                return 0

            if dz == 0:
                pltpu.make_async_copy(p.at[base + me], to, ret_sem.at[which]).start()
            lax.fori_loop(1 - dz, N, one, 0)

    loads[3].wait()
    loads[4].wait()
    experts(forward, r1, p1, pc, 0)
    give_back(p1, pc, ret1, 0)
    arrived(r1.at[pl.ds(0, 2 * N)], ssem.at[2])
    experts(backward, r2, r1, pc, 1)
    give_back(r1, pc, ret2, 1)

    gwin_parts, gwout_parts = (win0, win1, win2, win3, win4), (wout0, wout1, wout2, wout3, wout4)
    stores = []
    for m in range(5):
        if m >= 2:
            for copy in stores[m - 2]:
                copy.wait()
        slot = m % 2
        cut, wide = pl.ds(m * 128, 128), pl.ds(m * 256, 256)
        for ex in range(2):
            (eo, sg)[slot][ex] = dot(act[ex, :, cut], e2[ex], TN).astype(BF16)
            gwin[slot, ex] = dot(e1[ex, :, wide], pre[ex], TN).astype(BF16)
        copies = [
            pltpu.make_async_copy(gwin.at[slot], gwin_parts[m], w_sem.at[2 * m]),
            pltpu.make_async_copy((eo, sg)[slot], gwout_parts[m], w_sem.at[2 * m + 1]),
        ]
        for copy in copies:
            copy.start()
        stores.append(copies)

    def returned(ret, which):
        arrived(ret, ret_sem.at[which])
        return unpack_rows(ret[pl.ds(0, N)].astype(F32) + ret[pl.ds(N, N)].astype(F32)).astype(BF16)

    rows = returned(ret1, 0)
    for copy in stores[3] + stores[4]:
        copy.wait()
    for i in range(IMG):
        slots = dot(pick(i), rows).astype(BF16)
        c = com[:, image(i)]
        dc = dot(slots, g[image(i), :], NT)
        com[:, image(i)] = c * (dc - jnp.sum(c * dc, axis=0, keepdims=True))
        g[image(i), :] = dot(com_low[:, image(i)], slots, TN).astype(BF16)
        emit(g.at[image(i)], (mix0, mix1, mix2, mix3)[i], i)

    rows = returned(ret2, 1)
    for i in range(IMG):
        slots = dot(pick(i), rows).astype(BF16)
        sg[i // 2, EXP * (i % 2) : EXP * (i % 2 + 1), :] = slots
        d = dis[:, image(i)]
        dd = dot(slots, x[image(i), :], NT)
        term = d * (dd - jnp.sum(d * dd, axis=1, keepdims=True))
        lgrad[:, image(i)] = (com[:, image(i)] + term).astype(BF16)
    gd[...] = pack_rows(dot(lgrad[...], x[...]))

    block = (zhi * 2 + zlo) * 2 + core

    def near_device(k):
        zl, c, zh, b = near(k)
        return (zl * 2 + c, (xx * 4 + yy) * 2 + zh), b

    for k in range(1, 8):
        device, b = near_device(k)
        remote(gd.at[b], ar_a.at[k], ssem.at[8], ar_sem.at[0], device).start()

    def image_grad(i):
        left = jnp.concatenate([lgrad[:, image(i)], dis_low[:, image(i)]], axis=0)
        right = jnp.concatenate([wd[...], sg[i // 2, EXP * (i % 2) : EXP * (i % 2 + 1), :]], axis=0)
        x[image(i), :] = dot(left, right, TN).astype(BF16)
        emit(x.at[image(i)], (grad0, grad1, grad2, grad3)[i], 4 + i)

    image_grad(0)
    arrived(ar_a.at[pl.ds(1, 7)], ar_sem.at[0])
    total = gd[block].astype(F32)
    for k in range(1, 8):
        total += ar_a[k].astype(F32)
    ar_x[xx] = total.astype(BF16)
    for k in range(1, 4):
        remote(
            ar_x.at[xx], ar_x.at[xx], ssem.at[9], ar_sem.at[1], (group, (((xx + k) % 4) * 4 + yy) * 2 + zhi)
        ).start()

    def sum4(ref):
        return ((ref[0].astype(F32) + ref[1].astype(F32)) + (ref[2].astype(F32) + ref[3].astype(F32))).astype(BF16)

    image_grad(1)
    arrived(ar_x.at[pl.ds(0, 3)], ar_sem.at[1])
    ar_y[yy] = sum4(ar_x)
    for k in range(1, 4):
        remote(
            ar_y.at[yy], ar_y.at[yy], ssem.at[10], ar_sem.at[2], (group, (xx * 4 + (yy + k) % 4) * 2 + zhi)
        ).start()
    image_grad(2)
    arrived(ar_y.at[pl.ds(0, 3)], ar_sem.at[2])
    gdo[block] = sum4(ar_y)
    for k in range(1, 8):
        device, _ = near_device(k)
        remote(gdo.at[block], gdo.at[block], ssem.at[11], ar_sem.at[3], device).start()
    image_grad(3)
    arrived(gdo.at[pl.ds(0, 7)], ar_sem.at[3])
    emit(gdo, gd_out, 8)

    for which in range(2):
        arrived(r1.at[pl.ds(0, 2 * N - 1)], ssem.at[which])
        if which == 1:
            arrived(r1.at[pl.ds(0, 2 * N)], ssem.at[2 + which])
        arrived(r1.at[pl.ds(0, 2 * N)], ssem.at[4 + which])
        arrived(r1.at[pl.ds(0, 2 * N - 1)], ssem.at[6 + which])
    arrived(gd.at[pl.ds(0, 7)], ssem.at[8])
    arrived(ar_x.at[pl.ds(0, 3)], ssem.at[9])
    arrived(ar_y.at[pl.ds(0, 3)], ssem.at[10])
    arrived(gd.at[pl.ds(0, 7)], ssem.at[11])
    for copy in outs:
        copy.wait()


def finish(*refs):
    parts, (gd_in, mixed, gimg, gsum, gwin, gwout), (gd, wide, out_sem) = refs[:18], refs[18:24], refs[24:]
    load = pltpu.make_async_copy(gd_in, gd, out_sem.at[18])
    load.start()
    places = [mixed.at[pl.ds(i * TOK, TOK)] for i in range(IMG)] + [gimg.at[pl.ds(i * TOK, TOK)] for i in range(IMG)]
    places += [gwin.at[:, pl.ds(m * 256, 256)] for m in range(5)] + [gwout.at[:, pl.ds(m * 128, 128)] for m in range(5)]
    copies = [pltpu.make_async_copy(part, place, out_sem.at[k]) for k, (part, place) in enumerate(zip(parts, places))]
    for copy in copies:
        copy.start()
    load.wait()
    wide[...] = unpack_rows(gd[...].astype(F32))
    copies.append(pltpu.make_async_copy(wide, gsum, out_sem.at[19]))
    copies[-1].start()
    for copy in copies:
        copy.wait()


def per_device(images, dispatch_weight, weight_in, weight_out, out_grad):
    vmem = pltpu.VMEM
    message = (16, HALF)
    scratch = [
        vmem((T, D), BF16), vmem((EXP, D), BF16), vmem((2, D, HIDQ), BF16), vmem((2, HIDQ, D), BF16), vmem((T, D), BF16),
        vmem((N, *message), BF16), vmem((N, *message), BF16),
        vmem((4 * N, *message), BF16), vmem((4 * N, *message), BF16),
        vmem((2, 16 * N, D), BF16), vmem((2, 16 * N, D), BF16),
        vmem((2, 16 * N, HIDQ), BF16), vmem((2, 16 * N, HIDQ), BF16), vmem((2, 16 * N, HIDQ), BF16),
        vmem((4 * N, *message), BF16),
        vmem((2 * N, *message), BF16),
        vmem((2 * N, *message), BF16), vmem((2 * N, *message), BF16),
        vmem((EXP, T), F32), vmem((EXP, T), F32), vmem((EXP, T), BF16), vmem((EXP, T), BF16),
        vmem((ROWS, T), BF16),
        vmem((EXP, T), BF16), vmem((2, 2 * EXP, D), BF16), vmem((2, 2 * EXP, D), BF16),
        vmem((2, 2, 256, HIDQ), BF16),
        vmem((8, *message), BF16), vmem((8, *message), BF16), vmem((4, *message), BF16), vmem((4, *message), BF16),
        vmem((8, *message), BF16),
        pltpu.SemaphoreType.DMA((5,)), pltpu.SemaphoreType.DMA((9,)), pltpu.SemaphoreType.DMA((10,)),
        pltpu.SemaphoreType.DMA((12,)),
        pltpu.SemaphoreType.DMA((2, 2)), pltpu.SemaphoreType.DMA((2, 2)), pltpu.SemaphoreType.DMA((2, 2)),
        pltpu.SemaphoreType.DMA((2,)), pltpu.SemaphoreType.DMA((4,)),
    ]
    anywhere = pl.BlockSpec(memory_space=pl.ANY)
    tokens = jax.ShapeDtypeStruct((T, D), BF16)
    first, second = jax.ShapeDtypeStruct((2, D, HIDQ), BF16), jax.ShapeDtypeStruct((2, HIDQ, D), BF16)
    wd = dispatch_weight.T
    gd_shape = jax.ShapeDtypeStruct((8, *message), BF16)
    parts = pl.pallas_call(
        kernel,
        out_shape=(jax.ShapeDtypeStruct((TOK, D), BF16),) * 8
        + (jax.ShapeDtypeStruct((2, 256, HIDQ), BF16),) * 5
        + (jax.ShapeDtypeStruct((2, 128, D), BF16),) * 5
        + (gd_shape,),
        in_specs=[anywhere] * 5,
        out_specs=[anywhere] * 19,
        scratch_shapes=scratch,
        compiler_params=pltpu.CompilerParams(
            collective_id=0, has_side_effects=True, vmem_limit_bytes=LIMIT * 2**20
        ),
    )(images.reshape(T, D), wd, weight_in, weight_out, out_grad.reshape(T, D))
    mixed, gimg, gd, gwin, gwout = pl.pallas_call(
        finish,
        out_shape=(tokens, tokens, jax.ShapeDtypeStruct((EXP, D), F32), first, second),
        in_specs=[anywhere] * 19,
        out_specs=[anywhere] * 5,
        scratch_shapes=[vmem((8, *message), BF16), vmem((EXP, D), F32), pltpu.SemaphoreType.DMA((20,))],
        compiler_params=pltpu.CompilerParams(vmem_limit_bytes=12 * 2**20),
    )(*parts)
    return mixed.reshape(IMG, TOK, D), gimg.reshape(IMG, TOK, D), gd.T, gwin, gwout


def solution(mesh):
    tokens = P(("group", "expert"), None, None)
    first, second = P("expert", None, "group"), P("expert", "group", None)
    return jax.shard_map(
        per_device,
        mesh=mesh,
        in_specs=(tokens, P(), first, second, tokens),
        out_specs=(tokens, tokens, P(), first, second),
        check_vma=False,
    )
```

```python
import jax
import jax.numpy as jnp
from jax import lax
from jax.experimental import pallas as pl
from jax.experimental.pallas import tpu as pltpu
from jax.sharding import PartitionSpec as P

MESH = pl.DeviceIdType.MESH
LIMIT = 42
F32, BF16 = jnp.float32, jnp.bfloat16

D, HIDQ, TOK, IMG, EXP = 1280, 640, 256, 4, 64
ROWS = EXP * IMG
T = IMG * TOK
HALF = D // 2
N = 32
NT = (((1,), (1,)), ((), ()))
TN = (((0,), (0,)), ((), ()))


def dot(a, b, dims=(((1,), (0,)), ((), ()))):
    return lax.dot_general(a, b, dims, preferred_element_type=F32)


def gelu_pair(v):
    cdf = 0.5 * (1.0 + lax.erf(v * 0.7071067811865476))
    density = jnp.exp(-0.5 * v * v) * 0.3989422804014327
    return v * cdf, cdf + v * density


def pack_rows(rows):
    n = rows.shape[0] // 8
    left = rows[:, :HALF].reshape(n, 8, HALF)
    right = rows[:, HALF:].reshape(n, 8, HALF)
    return jnp.concatenate([left, right], axis=1).astype(BF16)


def unpack_rows(messages):
    n = messages.shape[0]
    left = messages[:, :8].reshape(8 * n, HALF)
    right = messages[:, 8:].reshape(8 * n, HALF)
    return jnp.concatenate([left, right], axis=1)


def low_rows(shape):
    return lax.broadcasted_iota(jnp.int32, shape, 1) < 4


def split_experts(messages):
    n = messages.shape[0] // 2
    parts = [[], []]
    for half in range(2):
        block = messages[:, 8 * half : 8 * half + 8].reshape(n, 2, 8, HALF)
        a, b = block[:, 0], block[:, 1]
        low = low_rows(a.shape)
        parts[0].append(jnp.where(low, a, pltpu.roll(b, 4, 1)).reshape(8 * n, HALF))
        parts[1].append(jnp.where(low, pltpu.roll(a, 4, 1), b).reshape(8 * n, HALF))
    return [jnp.concatenate(p, axis=1).astype(BF16) for p in parts]


def join_experts(first, second):
    n = first.shape[0] // 8
    halves = []
    for half in range(2):
        p0 = first[:, HALF * half : HALF * (half + 1)].reshape(n, 8, HALF)
        p1 = second[:, HALF * half : HALF * (half + 1)].reshape(n, 8, HALF)
        low = low_rows(p0.shape)
        a = jnp.where(low, p0, pltpu.roll(p1, 4, 1))
        b = jnp.where(low, pltpu.roll(p0, 4, 1), p1)
        halves.append(jnp.stack([a, b], axis=1).reshape(2 * n, 8, HALF))
    return jnp.concatenate(halves, axis=1).astype(BF16)


def kernel(
    x_hbm, wd_hbm, win_hbm, wout_hbm, g_hbm,
    mix0, mix1, mix2, mix3, grad0, grad1, grad2, grad3, win0, win1, win2, win3, win4, wout0, wout1, wout2, wout3, wout4,
    gd_out,
    x, wd, win, wout, g, send1, send2, r1, r2, e1, e2, act, slope, pre,
    p1, pc, ret1, ret2, dis, com, dis_low, com_low, spread_low, lgrad, eo, sg,
    gwin, gd, ar_a, ar_x, ar_y, gdo,
    in_sem, out_sem, w_sem, s_sem, ssem, d_sem, c_sem, b_sem, ret_sem, ar_sem,
):
    group, me = lax.axis_index("group"), lax.axis_index("expert")
    zlo, core = group // 2, group % 2
    xx, yy, zhi = me // 8, (me // 2) % 4, me % 2

    def far(dz, r):
        dx, dy, dh = r // 8, (r // 2) % 4, r % 2
        e = (((xx + dx) % 4) * 4 + (yy + dy) % 4) * 2 + (zhi + dh) % 2
        return (zlo + dz) % 2, e

    def near(k):
        dz, dc, dh = k // 4, (k // 2) % 2, k % 2
        zl, c, zh = (zlo + dz) % 2, (core + dc) % 2, (zhi + dh) % 2
        return zl, c, zh, (zh * 2 + zl) * 2 + c

    def remote(src, dst, send, recv, device):
        return pltpu.make_async_remote_copy(
            src_ref=src, dst_ref=dst, send_sem=send, recv_sem=recv, device_id=device, device_id_type=MESH
        )

    def arrived(ref, sem):
        pltpu.make_async_copy(ref, ref, sem).wait()

    partner = (zlo * 2 + 1 - core, me)

    loads = [
        pltpu.make_async_copy(src, dst, in_sem.at[k])
        for k, (src, dst) in enumerate(((wd_hbm, wd), (x_hbm, x), (g_hbm, g), (win_hbm, win), (wout_hbm, wout)))
    ]
    loads[0].start()
    loads[1].start()

    barrier = pltpu.get_barrier_semaphore()

    def greet(k, _):
        zl, e = far(k // N, k % N)
        pl.semaphore_signal(barrier, inc=1, device_id=(zl * 2 + core, e), device_id_type=MESH)
        return 0

    lax.fori_loop(1, 2 * N, greet, 0)
    pl.semaphore_signal(barrier, inc=1, device_id=partner, device_id_type=MESH)
    for dz, dh in ((0, 1), (1, 0), (1, 1)):
        e = (xx * 4 + yy) * 2 + (zhi + dh) % 2
        pl.semaphore_signal(
            barrier, inc=1, device_id=(((zlo + dz) % 2) * 2 + 1 - core, e), device_id_type=MESH
        )

    def image(i):
        return pl.ds(i * TOK, TOK)

    def pick(i):
        row = lax.broadcasted_iota(jnp.int32, (EXP, ROWS), 0)
        col = lax.broadcasted_iota(jnp.int32, (EXP, ROWS), 1)
        return jnp.where(col == row * IMG + i, 1.0, 0.0).astype(BF16)

    def spread(low, out):
        for i in range(IMG):
            out[:, image(i)] = dot(pick(i), low[:, image(i)], TN).astype(BF16)

    loads[0].wait()
    loads[1].wait()
    for load in loads[2:]:
        load.start()
    for i in range(IMG):
        scores = dot(wd[...], x[image(i), :], NT)
        com[:, image(i)] = scores
        up = jnp.exp(scores - jnp.max(scores, axis=1, keepdims=True))
        d = up / jnp.sum(up, axis=1, keepdims=True)
        dis[:, image(i)] = d
        dis_low[:, image(i)] = d.astype(BF16)
    spread(dis_low, spread_low)
    send1[...] = pack_rows(dot(spread_low[...], x[...]))
    pl.semaphore_wait(barrier, 2 * N - 1 + 4)

    def dispatch(send, rows, which):
        def one(k, _):
            zl, e = far(k // N, k % N)
            remote(
                send.at[e], rows.at[core * 2 * N + zlo * N + me], s_sem.at[which, k // N], d_sem.at[which, zlo],
                (zl * 2 + core, e),
            ).start()
            return 0

        pltpu.make_async_copy(send.at[me], rows.at[core * 2 * N + zlo * N + me], d_sem.at[which, zlo]).start()
        lax.fori_loop(1, 2 * N, one, 0)

    def left(which, dz):
        arrived(r1.at[pl.ds(0, N - 1 + dz)], s_sem.at[which, dz])

    dispatch(send1, r1, 0)
    for i in range(IMG):
        scores = com[:, image(i)]
        up = jnp.exp(scores - jnp.max(scores, axis=0, keepdims=True))
        c = up / jnp.sum(up, axis=0, keepdims=True)
        com[:, image(i)] = c
        com_low[:, image(i)] = c.astype(BF16)
    spread(com_low, spread_low)
    loads[2].wait()
    send2[...] = pack_rows(dot(spread_low[...], g[...]))
    left(0, 0)
    dispatch(send2, r2, 1)
    outs = []

    def emit(src, dst, k):
        copy = pltpu.make_async_copy(src, dst, out_sem.at[k])
        copy.start()
        outs.append(copy)


    def quarter(c, dz):
        return pl.ds(c * 2 * N + ((zlo + dz) % 2) * N, N)

    def per_expert(rows, out, c, dz, at):
        base = c * 2 * N + ((zlo + dz) % 2) * N

        def step(s, _):
            first, second = split_experts(rows[pl.ds(base + s * 8, 8)].astype(F32))
            to = pl.ds(pl.multiple_of(at * 4 * N + s * 32, 32), 32)
            out[0, to, :] = first
            out[1, to, :] = second
            return 0

        lax.fori_loop(0, N // 8, step, 0)

    def forward(c, dz, at):
        per_expert(r1, e1, c, dz, at)
        to = pl.ds(pl.multiple_of(at * 4 * N, 4 * N), 4 * N)
        partial = []
        for ex in range(2):
            value, grad = gelu_pair(dot(e1[ex, to, :], win[ex]))
            slope[ex, to, :] = grad.astype(BF16)
            low = value.astype(BF16)
            act[ex, to, :] = low
            partial.append(dot(low, wout[ex]))
        p1[quarter(c, dz)] = join_experts(*partial)

    def backward(c, dz, at):
        per_expert(r2, e2, c, dz, at)
        to = pl.ds(pl.multiple_of(at * 4 * N, 4 * N), 4 * N)
        partial = []
        for ex in range(2):
            low = (dot(e2[ex, to, :], wout[ex], NT) * slope[ex, to, :].astype(F32)).astype(BF16)
            pre[ex, to, :] = low
            partial.append(dot(low, win[ex], NT))
        r1[quarter(c, dz)] = join_experts(*partial)

    def experts(step, rows, p, pc, which):
        def part(dz, _):
            block = rows.at[quarter(core, dz)]
            arrived(block, d_sem.at[which, (zlo + dz) % 2])
            remote(block, block, ssem.at[2 + which], c_sem.at[which, dz], partner).start()
            step(core, dz, 2 * dz)
            theirs = quarter(1 - core, dz)
            arrived(rows.at[theirs], c_sem.at[which, dz])
            step(1 - core, dz, 2 * dz + 1)
            remote(
                p.at[theirs], pc.at[pl.ds(dz * N, N)], ssem.at[4 + which], b_sem.at[which, dz], partner
            ).start()
            return 0

        lax.fori_loop(0, 2, part, 0)

    def give_back(p, pc, ret, which):
        for dz in range(2):
            arrived(pc.at[pl.ds(dz * N, N)], b_sem.at[which, dz])
            zl = (zlo + dz) % 2
            base = core * 2 * N + zl * N

            def add(s, _):
                at = pl.ds(base + s * 8, 8)
                p[at] = (p[at].astype(F32) + pc[pl.ds(dz * N + s * 8, 8)].astype(F32)).astype(BF16)
                return 0

            lax.fori_loop(0, N // 8, add, 0)
            to = ret.at[zlo * N + me]

            def one(r, _):
                _, e = far(dz, r)
                remote(p.at[base + e], to, ssem.at[6 + which], ret_sem.at[which], (zl * 2 + core, e)).start()
                return 0

            if dz == 0:
                pltpu.make_async_copy(p.at[base + me], to, ret_sem.at[which]).start()
            lax.fori_loop(1 - dz, N, one, 0)

    loads[3].wait()
    loads[4].wait()
    experts(forward, r1, p1, pc, 0)
    left(1, 0)
    give_back(p1, pc, ret1, 0)
    arrived(r1.at[pl.ds(0, 2 * N)], ssem.at[2])
    experts(backward, r2, r1, pc, 1)
    give_back(r1, pc, ret2, 1)

    gwin_parts, gwout_parts = (win0, win1, win2, win3, win4), (wout0, wout1, wout2, wout3, wout4)
    stores = []
    for m in range(5):
        if m >= 2:
            for copy in stores[m - 2]:
                copy.wait()
        slot = m % 2
        cut, wide = pl.ds(m * 128, 128), pl.ds(m * 256, 256)
        for ex in range(2):
            (eo, sg)[slot][ex] = dot(act[ex, :, cut], e2[ex], TN).astype(BF16)
            gwin[slot, ex] = dot(e1[ex, :, wide], pre[ex], TN).astype(BF16)
        copies = [
            pltpu.make_async_copy(gwin.at[slot], gwin_parts[m], w_sem.at[2 * m]),
            pltpu.make_async_copy((eo, sg)[slot], gwout_parts[m], w_sem.at[2 * m + 1]),
        ]
        for copy in copies:
            copy.start()
        stores.append(copies)

    def returned(ret, which):
        arrived(ret, ret_sem.at[which])
        return unpack_rows(ret[pl.ds(0, N)].astype(F32) + ret[pl.ds(N, N)].astype(F32)).astype(BF16)

    rows = returned(ret1, 0)
    for copy in stores[3] + stores[4]:
        copy.wait()
    for i in range(IMG):
        slots = dot(pick(i), rows).astype(BF16)
        c = com[:, image(i)]
        dc = dot(slots, g[image(i), :], NT)
        com[:, image(i)] = c * (dc - jnp.sum(c * dc, axis=0, keepdims=True))
        g[image(i), :] = dot(com_low[:, image(i)], slots, TN).astype(BF16)
        emit(g.at[image(i)], (mix0, mix1, mix2, mix3)[i], i)

    rows = returned(ret2, 1)
    for i in range(IMG):
        slots = dot(pick(i), rows).astype(BF16)
        sg[i // 2, EXP * (i % 2) : EXP * (i % 2 + 1), :] = slots
        d = dis[:, image(i)]
        dd = dot(slots, x[image(i), :], NT)
        term = d * (dd - jnp.sum(d * dd, axis=1, keepdims=True))
        lgrad[:, image(i)] = (com[:, image(i)] + term).astype(BF16)
    gd[...] = pack_rows(dot(lgrad[...], x[...]))

    block = (zhi * 2 + zlo) * 2 + core

    def near_device(k):
        zl, c, zh, b = near(k)
        return (zl * 2 + c, (xx * 4 + yy) * 2 + zh), b

    for k in range(1, 8):
        device, b = near_device(k)
        remote(gd.at[b], ar_a.at[k], ssem.at[8], ar_sem.at[0], device).start()

    def image_grad(i):
        left = jnp.concatenate([lgrad[:, image(i)], dis_low[:, image(i)]], axis=0)
        right = jnp.concatenate([wd[...], sg[i // 2, EXP * (i % 2) : EXP * (i % 2 + 1), :]], axis=0)
        x[image(i), :] = dot(left, right, TN).astype(BF16)
        emit(x.at[image(i)], (grad0, grad1, grad2, grad3)[i], 4 + i)

    image_grad(0)
    arrived(ar_a.at[pl.ds(1, 7)], ar_sem.at[0])
    total = gd[block].astype(F32)
    for k in range(1, 8):
        total += ar_a[k].astype(F32)
    ar_x[xx] = total.astype(BF16)
    for k in range(1, 4):
        remote(
            ar_x.at[xx], ar_x.at[xx], ssem.at[9], ar_sem.at[1], (group, (((xx + k) % 4) * 4 + yy) * 2 + zhi)
        ).start()

    def sum4(ref):
        return ((ref[0].astype(F32) + ref[1].astype(F32)) + (ref[2].astype(F32) + ref[3].astype(F32))).astype(BF16)

    image_grad(1)
    arrived(ar_x.at[pl.ds(0, 3)], ar_sem.at[1])
    ar_y[yy] = sum4(ar_x)
    for k in range(1, 4):
        remote(
            ar_y.at[yy], ar_y.at[yy], ssem.at[10], ar_sem.at[2], (group, (xx * 4 + (yy + k) % 4) * 2 + zhi)
        ).start()
    image_grad(2)
    arrived(ar_y.at[pl.ds(0, 3)], ar_sem.at[2])
    gdo[block] = sum4(ar_y)
    for k in range(1, 8):
        device, _ = near_device(k)
        remote(gdo.at[block], gdo.at[block], ssem.at[11], ar_sem.at[3], device).start()
    image_grad(3)
    arrived(gdo.at[pl.ds(0, 7)], ar_sem.at[3])
    emit(gdo, gd_out, 8)

    for which in range(2):
        left(which, 1)
        if which == 1:
            arrived(r1.at[pl.ds(0, 2 * N)], ssem.at[2 + which])
        arrived(r1.at[pl.ds(0, 2 * N)], ssem.at[4 + which])
        arrived(r1.at[pl.ds(0, 2 * N - 1)], ssem.at[6 + which])
    arrived(gd.at[pl.ds(0, 7)], ssem.at[8])
    arrived(ar_x.at[pl.ds(0, 3)], ssem.at[9])
    arrived(ar_y.at[pl.ds(0, 3)], ssem.at[10])
    arrived(gd.at[pl.ds(0, 7)], ssem.at[11])
    for copy in outs:
        copy.wait()


def finish(*refs):
    parts, (gd_in, mixed, gimg, gsum, gwin, gwout), (gd, wide, out_sem) = refs[:18], refs[18:24], refs[24:]
    load = pltpu.make_async_copy(gd_in, gd, out_sem.at[18])
    load.start()
    places = [mixed.at[pl.ds(i * TOK, TOK)] for i in range(IMG)] + [gimg.at[pl.ds(i * TOK, TOK)] for i in range(IMG)]
    places += [gwin.at[:, pl.ds(m * 256, 256)] for m in range(5)] + [gwout.at[:, pl.ds(m * 128, 128)] for m in range(5)]
    copies = [pltpu.make_async_copy(part, place, out_sem.at[k]) for k, (part, place) in enumerate(zip(parts, places))]
    for copy in copies:
        copy.start()
    load.wait()
    wide[...] = unpack_rows(gd[...].astype(F32))
    copies.append(pltpu.make_async_copy(wide, gsum, out_sem.at[19]))
    copies[-1].start()
    for copy in copies:
        copy.wait()


def per_device(images, dispatch_weight, weight_in, weight_out, out_grad):
    vmem = pltpu.VMEM
    message = (16, HALF)
    scratch = [
        vmem((T, D), BF16), vmem((EXP, D), BF16), vmem((2, D, HIDQ), BF16), vmem((2, HIDQ, D), BF16), vmem((T, D), BF16),
        vmem((N, *message), BF16), vmem((N, *message), BF16),
        vmem((4 * N, *message), BF16), vmem((4 * N, *message), BF16),
        vmem((2, 16 * N, D), BF16), vmem((2, 16 * N, D), BF16),
        vmem((2, 16 * N, HIDQ), BF16), vmem((2, 16 * N, HIDQ), BF16), vmem((2, 16 * N, HIDQ), BF16),
        vmem((4 * N, *message), BF16),
        vmem((2 * N, *message), BF16),
        vmem((2 * N, *message), BF16), vmem((2 * N, *message), BF16),
        vmem((EXP, T), F32), vmem((EXP, T), F32), vmem((EXP, T), BF16), vmem((EXP, T), BF16),
        vmem((ROWS, T), BF16),
        vmem((EXP, T), BF16), vmem((2, 2 * EXP, D), BF16), vmem((2, 2 * EXP, D), BF16),
        vmem((2, 2, 256, HIDQ), BF16),
        vmem((8, *message), BF16), vmem((8, *message), BF16), vmem((4, *message), BF16), vmem((4, *message), BF16),
        vmem((8, *message), BF16),
        pltpu.SemaphoreType.DMA((5,)), pltpu.SemaphoreType.DMA((9,)), pltpu.SemaphoreType.DMA((10,)), pltpu.SemaphoreType.DMA((2, 2)),
        pltpu.SemaphoreType.DMA((12,)),
        pltpu.SemaphoreType.DMA((2, 2)), pltpu.SemaphoreType.DMA((2, 2)), pltpu.SemaphoreType.DMA((2, 2)),
        pltpu.SemaphoreType.DMA((2,)), pltpu.SemaphoreType.DMA((4,)),
    ]
    anywhere = pl.BlockSpec(memory_space=pl.ANY)
    tokens = jax.ShapeDtypeStruct((T, D), BF16)
    first, second = jax.ShapeDtypeStruct((2, D, HIDQ), BF16), jax.ShapeDtypeStruct((2, HIDQ, D), BF16)
    wd = dispatch_weight.T
    gd_shape = jax.ShapeDtypeStruct((8, *message), BF16)
    parts = pl.pallas_call(
        kernel,
        out_shape=(jax.ShapeDtypeStruct((TOK, D), BF16),) * 8
        + (jax.ShapeDtypeStruct((2, 256, HIDQ), BF16),) * 5
        + (jax.ShapeDtypeStruct((2, 128, D), BF16),) * 5
        + (gd_shape,),
        in_specs=[anywhere] * 5,
        out_specs=[anywhere] * 19,
        scratch_shapes=scratch,
        compiler_params=pltpu.CompilerParams(
            collective_id=0, has_side_effects=True, vmem_limit_bytes=LIMIT * 2**20
        ),
    )(images.reshape(T, D), wd, weight_in, weight_out, out_grad.reshape(T, D))
    mixed, gimg, gd, gwin, gwout = pl.pallas_call(
        finish,
        out_shape=(tokens, tokens, jax.ShapeDtypeStruct((EXP, D), F32), first, second),
        in_specs=[anywhere] * 19,
        out_specs=[anywhere] * 5,
        scratch_shapes=[vmem((8, *message), BF16), vmem((EXP, D), F32), pltpu.SemaphoreType.DMA((20,))],
        compiler_params=pltpu.CompilerParams(vmem_limit_bytes=12 * 2**20),
    )(*parts)
    return mixed.reshape(IMG, TOK, D), gimg.reshape(IMG, TOK, D), gd.T, gwin, gwout


def solution(mesh):
    tokens = P(("group", "expert"), None, None)
    first, second = P("expert", None, "group"), P("expert", "group", None)
    return jax.shard_map(
        per_device,
        mesh=mesh,
        in_specs=(tokens, P(), first, second, tokens),
        out_specs=(tokens, tokens, P(), first, second),
        check_vma=False,
    )
```

```python
import jax
import jax.numpy as jnp
from jax import lax
from jax.experimental import pallas as pl
from jax.experimental.pallas import tpu as pltpu
from jax.sharding import PartitionSpec as P

MESH = pl.DeviceIdType.MESH
LIMIT = 42
F32, BF16 = jnp.float32, jnp.bfloat16

D, HIDQ, TOK, IMG, EXP = 1280, 640, 256, 4, 64
ROWS = EXP * IMG
T = IMG * TOK
HALF = D // 2
N = 32
NT = (((1,), (1,)), ((), ()))
TN = (((0,), (0,)), ((), ()))


def dot(a, b, dims=(((1,), (0,)), ((), ()))):
    return lax.dot_general(a, b, dims, preferred_element_type=F32)


def gelu_pair(v):
    cdf = 0.5 * (1.0 + lax.erf(v * 0.7071067811865476))
    density = jnp.exp(-0.5 * v * v) * 0.3989422804014327
    return v * cdf, cdf + v * density


def pack_rows(rows):
    n = rows.shape[0] // 8
    left = rows[:, :HALF].reshape(n, 8, HALF)
    right = rows[:, HALF:].reshape(n, 8, HALF)
    return jnp.concatenate([left, right], axis=1).astype(BF16)


def unpack_rows(messages):
    n = messages.shape[0]
    left = messages[:, :8].reshape(8 * n, HALF)
    right = messages[:, 8:].reshape(8 * n, HALF)
    return jnp.concatenate([left, right], axis=1)


def low_rows(shape):
    return lax.broadcasted_iota(jnp.int32, shape, 1) < 4


def split_experts(messages):
    n = messages.shape[0] // 2
    parts = [[], []]
    for half in range(2):
        block = messages[:, 8 * half : 8 * half + 8].reshape(n, 2, 8, HALF)
        a, b = block[:, 0], block[:, 1]
        low = low_rows(a.shape)
        parts[0].append(jnp.where(low, a, pltpu.roll(b, 4, 1)).reshape(8 * n, HALF))
        parts[1].append(jnp.where(low, pltpu.roll(a, 4, 1), b).reshape(8 * n, HALF))
    return [jnp.concatenate(p, axis=1).astype(BF16) for p in parts]


def join_experts(first, second):
    n = first.shape[0] // 8
    halves = []
    for half in range(2):
        p0 = first[:, HALF * half : HALF * (half + 1)].reshape(n, 8, HALF)
        p1 = second[:, HALF * half : HALF * (half + 1)].reshape(n, 8, HALF)
        low = low_rows(p0.shape)
        a = jnp.where(low, p0, pltpu.roll(p1, 4, 1))
        b = jnp.where(low, pltpu.roll(p0, 4, 1), p1)
        halves.append(jnp.stack([a, b], axis=1).reshape(2 * n, 8, HALF))
    return jnp.concatenate(halves, axis=1).astype(BF16)


def kernel(
    x_hbm, wd_hbm, win_hbm, wout_hbm, g_hbm,
    mix0, mix1, mix2, mix3, grad0, grad1, grad2, grad3, win0, win1, win2, win3, win4, wout0, wout1, wout2, wout3, wout4,
    gd_out,
    x, wd, win, wout, g, send1, send2, r1, r2, e1, e2, act, slope, pre,
    p1, pc, ret1, ret2, dis, com, dis_low, com_low, spread_low, lgrad, eo, sg,
    gwin, gd, ar_a, ar_x, ar_y, gdo,
    in_sem, out_sem, w_sem, s_sem, ssem, d_sem, c_sem, b_sem, ret_sem, ar_sem,
):
    group, me = lax.axis_index("group"), lax.axis_index("expert")
    zlo, core = group // 2, group % 2
    xx, yy, zhi = me // 8, (me // 2) % 4, me % 2

    def far(dz, r):
        dx, dy, dh = r // 8, (r // 2) % 4, r % 2
        e = (((xx + dx) % 4) * 4 + (yy + dy) % 4) * 2 + (zhi + dh) % 2
        return (zlo + dz) % 2, e

    def near(k):
        dz, dc, dh = k // 4, (k // 2) % 2, k % 2
        zl, c, zh = (zlo + dz) % 2, (core + dc) % 2, (zhi + dh) % 2
        return zl, c, zh, (zh * 2 + zl) * 2 + c

    def remote(src, dst, send, recv, device):
        return pltpu.make_async_remote_copy(
            src_ref=src, dst_ref=dst, send_sem=send, recv_sem=recv, device_id=device, device_id_type=MESH
        )

    def arrived(ref, sem):
        pltpu.make_async_copy(ref, ref, sem).wait()

    partner = (zlo * 2 + 1 - core, me)

    loads = [
        pltpu.make_async_copy(src, dst, in_sem.at[k])
        for k, (src, dst) in enumerate(((wd_hbm, wd), (x_hbm, x), (g_hbm, g), (win_hbm, win), (wout_hbm, wout)))
    ]
    loads[0].start()
    loads[1].start()

    barrier = pltpu.get_barrier_semaphore()

    def greet(k, _):
        zl, e = far(k // N, k % N)
        pl.semaphore_signal(barrier, inc=1, device_id=(zl * 2 + core, e), device_id_type=MESH)
        return 0

    lax.fori_loop(1, 2 * N, greet, 0)
    pl.semaphore_signal(barrier, inc=1, device_id=partner, device_id_type=MESH)
    for dz, dh in ((0, 1), (1, 0), (1, 1)):
        e = (xx * 4 + yy) * 2 + (zhi + dh) % 2
        pl.semaphore_signal(
            barrier, inc=1, device_id=(((zlo + dz) % 2) * 2 + 1 - core, e), device_id_type=MESH
        )

    def image(i):
        return pl.ds(i * TOK, TOK)

    def pick(i):
        row = lax.broadcasted_iota(jnp.int32, (EXP, ROWS), 0)
        col = lax.broadcasted_iota(jnp.int32, (EXP, ROWS), 1)
        return jnp.where(col == row * IMG + i, 1.0, 0.0).astype(BF16)

    def spread(low, out):
        for i in range(IMG):
            out[:, image(i)] = dot(pick(i), low[:, image(i)], TN).astype(BF16)

    loads[0].wait()
    loads[1].wait()
    for load in loads[2:]:
        load.start()
    for i in range(IMG):
        scores = dot(wd[...], x[image(i), :], NT)
        com[:, image(i)] = scores
        up = jnp.exp(scores - jnp.max(scores, axis=1, keepdims=True))
        d = up / jnp.sum(up, axis=1, keepdims=True)
        dis[:, image(i)] = d
        dis_low[:, image(i)] = d.astype(BF16)
    spread(dis_low, spread_low)
    send1[...] = pack_rows(dot(spread_low[...], x[...]))
    pl.semaphore_wait(barrier, 2 * N - 1 + 4)

    def dispatch(send, rows, which):
        def one(k, _):
            zl, e = far(k // N, k % N)
            remote(
                send.at[e], rows.at[core * 2 * N + zlo * N + me], s_sem.at[which, k // N], d_sem.at[which, zlo],
                (zl * 2 + core, e),
            ).start()
            return 0

        pltpu.make_async_copy(send.at[me], rows.at[core * 2 * N + zlo * N + me], d_sem.at[which, zlo]).start()
        lax.fori_loop(1, 2 * N, one, 0)

    def left(which, dz):
        arrived(r1.at[pl.ds(0, N - 1 + dz)], s_sem.at[which, dz])

    dispatch(send1, r1, 0)
    for i in range(IMG):
        scores = com[:, image(i)]
        up = jnp.exp(scores - jnp.max(scores, axis=0, keepdims=True))
        c = up / jnp.sum(up, axis=0, keepdims=True)
        com[:, image(i)] = c
        com_low[:, image(i)] = c.astype(BF16)
    spread(com_low, spread_low)
    loads[2].wait()
    send2[...] = pack_rows(dot(spread_low[...], g[...]))
    left(0, 0)
    dispatch(send2, r2, 1)
    outs = []

    def emit(src, dst, k):
        copy = pltpu.make_async_copy(src, dst, out_sem.at[k])
        copy.start()
        outs.append(copy)


    def quarter(c, dz):
        return pl.ds(c * 2 * N + ((zlo + dz) % 2) * N, N)

    def per_expert(rows, out, c, dz, at):
        base = c * 2 * N + ((zlo + dz) % 2) * N

        def step(s, _):
            first, second = split_experts(rows[pl.ds(base + s * 8, 8)].astype(F32))
            to = pl.ds(pl.multiple_of(at * 4 * N + s * 32, 32), 32)
            out[0, to, :] = first
            out[1, to, :] = second
            return 0

        lax.fori_loop(0, N // 8, step, 0)

    def forward(c, dz, at):
        per_expert(r1, e1, c, dz, at)
        to = pl.ds(pl.multiple_of(at * 4 * N, 4 * N), 4 * N)
        partial = []
        for ex in range(2):
            value, grad = gelu_pair(dot(e1[ex, to, :], win[ex]))
            slope[ex, to, :] = grad.astype(BF16)
            low = value.astype(BF16)
            act[ex, to, :] = low
            partial.append(dot(low, wout[ex]))
        p1[quarter(c, dz)] = join_experts(*partial)

    def backward(c, dz, at):
        per_expert(r2, e2, c, dz, at)
        to = pl.ds(pl.multiple_of(at * 4 * N, 4 * N), 4 * N)
        partial = []
        for ex in range(2):
            low = (dot(e2[ex, to, :], wout[ex], NT) * slope[ex, to, :].astype(F32)).astype(BF16)
            pre[ex, to, :] = low
            partial.append(dot(low, win[ex], NT))
        r1[quarter(c, dz)] = join_experts(*partial)

    def give_back(p, pc, ret, which, dz):
        arrived(pc.at[pl.ds(dz * N, N)], b_sem.at[which, dz])
        zl = (zlo + dz) % 2
        base = core * 2 * N + zl * N

        def add(s, _):
            at = pl.ds(base + s * 8, 8)
            p[at] = (p[at].astype(F32) + pc[pl.ds(dz * N + s * 8, 8)].astype(F32)).astype(BF16)
            return 0

        lax.fori_loop(0, N // 8, add, 0)
        to = ret.at[zlo * N + me]

        def one(r, _):
            _, e = far(dz, r)
            remote(p.at[base + e], to, ssem.at[6 + which], ret_sem.at[which], (zl * 2 + core, e)).start()
            return 0

        if dz == 0:
            pltpu.make_async_copy(p.at[base + me], to, ret_sem.at[which]).start()
        lax.fori_loop(1 - dz, N, one, 0)

    def experts(step, rows, p, pc, ret, which):
        def part(dz, _):
            block = rows.at[quarter(core, dz)]
            arrived(block, d_sem.at[which, (zlo + dz) % 2])
            remote(block, block, ssem.at[2 + which], c_sem.at[which, dz], partner).start()
            step(core, dz, 2 * dz)

            @pl.when(dz == 1)
            def _():
                give_back(p, pc, ret, which, 0)

            theirs = quarter(1 - core, dz)
            arrived(rows.at[theirs], c_sem.at[which, dz])
            step(1 - core, dz, 2 * dz + 1)
            remote(
                p.at[theirs], pc.at[pl.ds(dz * N, N)], ssem.at[4 + which], b_sem.at[which, dz], partner
            ).start()
            return 0

        lax.fori_loop(0, 2, part, 0)
        give_back(p, pc, ret, which, 1)

    loads[3].wait()
    loads[4].wait()
    experts(forward, r1, p1, pc, ret1, 0)
    arrived(r1.at[pl.ds(0, 2 * N)], ssem.at[2])
    experts(backward, r2, r1, pc, ret2, 1)

    gwin_parts, gwout_parts = (win0, win1, win2, win3, win4), (wout0, wout1, wout2, wout3, wout4)
    stores = []
    for m in range(5):
        if m >= 2:
            for copy in stores[m - 2]:
                copy.wait()
        slot = m % 2
        cut, wide = pl.ds(m * 128, 128), pl.ds(m * 256, 256)
        for ex in range(2):
            (eo, sg)[slot][ex] = dot(act[ex, :, cut], e2[ex], TN).astype(BF16)
            gwin[slot, ex] = dot(e1[ex, :, wide], pre[ex], TN).astype(BF16)
        copies = [
            pltpu.make_async_copy(gwin.at[slot], gwin_parts[m], w_sem.at[2 * m]),
            pltpu.make_async_copy((eo, sg)[slot], gwout_parts[m], w_sem.at[2 * m + 1]),
        ]
        for copy in copies:
            copy.start()
        stores.append(copies)

    def returned(ret, which):
        arrived(ret, ret_sem.at[which])
        return unpack_rows(ret[pl.ds(0, N)].astype(F32) + ret[pl.ds(N, N)].astype(F32)).astype(BF16)

    rows = returned(ret1, 0)
    for copy in stores[3] + stores[4]:
        copy.wait()
    for i in range(IMG):
        slots = dot(pick(i), rows).astype(BF16)
        c = com[:, image(i)]
        dc = dot(slots, g[image(i), :], NT)
        com[:, image(i)] = c * (dc - jnp.sum(c * dc, axis=0, keepdims=True))
        g[image(i), :] = dot(com_low[:, image(i)], slots, TN).astype(BF16)
        emit(g.at[image(i)], (mix0, mix1, mix2, mix3)[i], i)

    rows = returned(ret2, 1)
    for i in range(IMG):
        slots = dot(pick(i), rows).astype(BF16)
        sg[i // 2, EXP * (i % 2) : EXP * (i % 2 + 1), :] = slots
        d = dis[:, image(i)]
        dd = dot(slots, x[image(i), :], NT)
        term = d * (dd - jnp.sum(d * dd, axis=1, keepdims=True))
        lgrad[:, image(i)] = (com[:, image(i)] + term).astype(BF16)
    gd[...] = pack_rows(dot(lgrad[...], x[...]))

    block = (zhi * 2 + zlo) * 2 + core

    def near_device(k):
        zl, c, zh, b = near(k)
        return (zl * 2 + c, (xx * 4 + yy) * 2 + zh), b

    for k in range(1, 8):
        device, b = near_device(k)
        remote(gd.at[b], ar_a.at[k], ssem.at[8], ar_sem.at[0], device).start()

    def image_grad(i):
        left = jnp.concatenate([lgrad[:, image(i)], dis_low[:, image(i)]], axis=0)
        right = jnp.concatenate([wd[...], sg[i // 2, EXP * (i % 2) : EXP * (i % 2 + 1), :]], axis=0)
        x[image(i), :] = dot(left, right, TN).astype(BF16)
        emit(x.at[image(i)], (grad0, grad1, grad2, grad3)[i], 4 + i)

    image_grad(0)
    arrived(ar_a.at[pl.ds(1, 7)], ar_sem.at[0])
    total = gd[block].astype(F32)
    for k in range(1, 8):
        total += ar_a[k].astype(F32)
    ar_x[xx] = total.astype(BF16)
    for k in range(1, 4):
        remote(
            ar_x.at[xx], ar_x.at[xx], ssem.at[9], ar_sem.at[1], (group, (((xx + k) % 4) * 4 + yy) * 2 + zhi)
        ).start()

    def sum4(ref):
        return ((ref[0].astype(F32) + ref[1].astype(F32)) + (ref[2].astype(F32) + ref[3].astype(F32))).astype(BF16)

    image_grad(1)
    arrived(ar_x.at[pl.ds(0, 3)], ar_sem.at[1])
    ar_y[yy] = sum4(ar_x)
    for k in range(1, 4):
        remote(
            ar_y.at[yy], ar_y.at[yy], ssem.at[10], ar_sem.at[2], (group, (xx * 4 + (yy + k) % 4) * 2 + zhi)
        ).start()
    image_grad(2)
    arrived(ar_y.at[pl.ds(0, 3)], ar_sem.at[2])
    gdo[block] = sum4(ar_y)
    for k in range(1, 8):
        device, _ = near_device(k)
        remote(gdo.at[block], gdo.at[block], ssem.at[11], ar_sem.at[3], device).start()
    image_grad(3)
    arrived(gdo.at[pl.ds(0, 7)], ar_sem.at[3])
    emit(gdo, gd_out, 8)

    for which in range(2):
        left(which, 1)
        if which == 1:
            left(which, 0)
        if which == 1:
            arrived(r1.at[pl.ds(0, 2 * N)], ssem.at[2 + which])
        arrived(r1.at[pl.ds(0, 2 * N)], ssem.at[4 + which])
        arrived(r1.at[pl.ds(0, 2 * N - 1)], ssem.at[6 + which])
    arrived(gd.at[pl.ds(0, 7)], ssem.at[8])
    arrived(ar_x.at[pl.ds(0, 3)], ssem.at[9])
    arrived(ar_y.at[pl.ds(0, 3)], ssem.at[10])
    arrived(gd.at[pl.ds(0, 7)], ssem.at[11])
    for copy in outs:
        copy.wait()


def finish(*refs):
    parts, (gd_in, mixed, gimg, gsum, gwin, gwout), (gd, wide, out_sem) = refs[:18], refs[18:24], refs[24:]
    load = pltpu.make_async_copy(gd_in, gd, out_sem.at[18])
    load.start()
    places = [mixed.at[pl.ds(i * TOK, TOK)] for i in range(IMG)] + [gimg.at[pl.ds(i * TOK, TOK)] for i in range(IMG)]
    places += [gwin.at[:, pl.ds(m * 256, 256)] for m in range(5)] + [gwout.at[:, pl.ds(m * 128, 128)] for m in range(5)]
    copies = [pltpu.make_async_copy(part, place, out_sem.at[k]) for k, (part, place) in enumerate(zip(parts, places))]
    for copy in copies:
        copy.start()
    load.wait()
    wide[...] = unpack_rows(gd[...].astype(F32))
    copies.append(pltpu.make_async_copy(wide, gsum, out_sem.at[19]))
    copies[-1].start()
    for copy in copies:
        copy.wait()


def per_device(images, dispatch_weight, weight_in, weight_out, out_grad):
    vmem = pltpu.VMEM
    message = (16, HALF)
    scratch = [
        vmem((T, D), BF16), vmem((EXP, D), BF16), vmem((2, D, HIDQ), BF16), vmem((2, HIDQ, D), BF16), vmem((T, D), BF16),
        vmem((N, *message), BF16), vmem((N, *message), BF16),
        vmem((4 * N, *message), BF16), vmem((4 * N, *message), BF16),
        vmem((2, 16 * N, D), BF16), vmem((2, 16 * N, D), BF16),
        vmem((2, 16 * N, HIDQ), BF16), vmem((2, 16 * N, HIDQ), BF16), vmem((2, 16 * N, HIDQ), BF16),
        vmem((4 * N, *message), BF16),
        vmem((2 * N, *message), BF16),
        vmem((2 * N, *message), BF16), vmem((2 * N, *message), BF16),
        vmem((EXP, T), F32), vmem((EXP, T), F32), vmem((EXP, T), BF16), vmem((EXP, T), BF16),
        vmem((ROWS, T), BF16),
        vmem((EXP, T), BF16), vmem((2, 2 * EXP, D), BF16), vmem((2, 2 * EXP, D), BF16),
        vmem((2, 2, 256, HIDQ), BF16),
        vmem((8, *message), BF16), vmem((8, *message), BF16), vmem((4, *message), BF16), vmem((4, *message), BF16),
        vmem((8, *message), BF16),
        pltpu.SemaphoreType.DMA((5,)), pltpu.SemaphoreType.DMA((9,)), pltpu.SemaphoreType.DMA((10,)), pltpu.SemaphoreType.DMA((2, 2)),
        pltpu.SemaphoreType.DMA((12,)),
        pltpu.SemaphoreType.DMA((2, 2)), pltpu.SemaphoreType.DMA((2, 2)), pltpu.SemaphoreType.DMA((2, 2)),
        pltpu.SemaphoreType.DMA((2,)), pltpu.SemaphoreType.DMA((4,)),
    ]
    anywhere = pl.BlockSpec(memory_space=pl.ANY)
    tokens = jax.ShapeDtypeStruct((T, D), BF16)
    first, second = jax.ShapeDtypeStruct((2, D, HIDQ), BF16), jax.ShapeDtypeStruct((2, HIDQ, D), BF16)
    wd = dispatch_weight.T
    gd_shape = jax.ShapeDtypeStruct((8, *message), BF16)
    parts = pl.pallas_call(
        kernel,
        out_shape=(jax.ShapeDtypeStruct((TOK, D), BF16),) * 8
        + (jax.ShapeDtypeStruct((2, 256, HIDQ), BF16),) * 5
        + (jax.ShapeDtypeStruct((2, 128, D), BF16),) * 5
        + (gd_shape,),
        in_specs=[anywhere] * 5,
        out_specs=[anywhere] * 19,
        scratch_shapes=scratch,
        compiler_params=pltpu.CompilerParams(
            collective_id=0, has_side_effects=True, vmem_limit_bytes=LIMIT * 2**20
        ),
    )(images.reshape(T, D), wd, weight_in, weight_out, out_grad.reshape(T, D))
    mixed, gimg, gd, gwin, gwout = pl.pallas_call(
        finish,
        out_shape=(tokens, tokens, jax.ShapeDtypeStruct((EXP, D), F32), first, second),
        in_specs=[anywhere] * 19,
        out_specs=[anywhere] * 5,
        scratch_shapes=[vmem((8, *message), BF16), vmem((EXP, D), F32), pltpu.SemaphoreType.DMA((20,))],
        compiler_params=pltpu.CompilerParams(vmem_limit_bytes=12 * 2**20),
    )(*parts)
    return mixed.reshape(IMG, TOK, D), gimg.reshape(IMG, TOK, D), gd.T, gwin, gwout


def solution(mesh):
    tokens = P(("group", "expert"), None, None)
    first, second = P("expert", None, "group"), P("expert", "group", None)
    return jax.shard_map(
        per_device,
        mesh=mesh,
        in_specs=(tokens, P(), first, second, tokens),
        out_specs=(tokens, tokens, P(), first, second),
        check_vma=False,
    )
```

```python
import jax
import jax.numpy as jnp
from jax import lax
from jax.experimental import pallas as pl
from jax.experimental.pallas import tpu as pltpu
from jax.sharding import PartitionSpec as P

MESH = pl.DeviceIdType.MESH
LIMIT = 42
F32, BF16 = jnp.float32, jnp.bfloat16

D, HIDQ, TOK, IMG, EXP = 1280, 640, 256, 4, 64
ROWS = EXP * IMG
T = IMG * TOK
HALF = D // 2
N = 32
NT = (((1,), (1,)), ((), ()))
TN = (((0,), (0,)), ((), ()))


def dot(a, b, dims=(((1,), (0,)), ((), ()))):
    return lax.dot_general(a, b, dims, preferred_element_type=F32)


def gelu_pair(v):
    cdf = 0.5 * (1.0 + lax.erf(v * 0.7071067811865476))
    density = jnp.exp(-0.5 * v * v) * 0.3989422804014327
    return v * cdf, cdf + v * density


def pack_rows(rows):
    n = rows.shape[0] // 8
    left = rows[:, :HALF].reshape(n, 8, HALF)
    right = rows[:, HALF:].reshape(n, 8, HALF)
    return jnp.concatenate([left, right], axis=1).astype(BF16)


def unpack_rows(messages):
    n = messages.shape[0]
    left = messages[:, :8].reshape(8 * n, HALF)
    right = messages[:, 8:].reshape(8 * n, HALF)
    return jnp.concatenate([left, right], axis=1)


def low_rows(shape):
    return lax.broadcasted_iota(jnp.int32, shape, 1) < 4


def split_experts(messages):
    n = messages.shape[0] // 2
    parts = [[], []]
    for half in range(2):
        block = messages[:, 8 * half : 8 * half + 8].reshape(n, 2, 8, HALF)
        a, b = block[:, 0], block[:, 1]
        low = low_rows(a.shape)
        parts[0].append(jnp.where(low, a, pltpu.roll(b, 4, 1)).reshape(8 * n, HALF))
        parts[1].append(jnp.where(low, pltpu.roll(a, 4, 1), b).reshape(8 * n, HALF))
    return [jnp.concatenate(p, axis=1).astype(BF16) for p in parts]


def join_experts(first, second):
    n = first.shape[0] // 8
    halves = []
    for half in range(2):
        p0 = first[:, HALF * half : HALF * (half + 1)].reshape(n, 8, HALF)
        p1 = second[:, HALF * half : HALF * (half + 1)].reshape(n, 8, HALF)
        low = low_rows(p0.shape)
        a = jnp.where(low, p0, pltpu.roll(p1, 4, 1))
        b = jnp.where(low, pltpu.roll(p0, 4, 1), p1)
        halves.append(jnp.stack([a, b], axis=1).reshape(2 * n, 8, HALF))
    return jnp.concatenate(halves, axis=1).astype(BF16)


def kernel(
    x_hbm, wd_hbm, win_hbm, wout_hbm, g_hbm,
    mix0, mix1, mix2, mix3, grad0, grad1, grad2, grad3, win0, win1, win2, win3, win4, wout0, wout1, wout2, wout3, wout4,
    gd_out,
    x, wd, win, wout, g, send1, send2, r1, r2, e1, e2, act, slope, pre,
    p1, pc, ret1, ret2, dis, com, dis_low, com_low, spread_low, lgrad, eo, sg,
    gwin, gd, ar_a, ar_x, ar_y, gdo,
    in_sem, out_sem, w_sem, s_sem, ssem, d_sem, c_sem, b_sem, ret_sem, ar_sem,
):
    group, me = lax.axis_index("group"), lax.axis_index("expert")
    zlo, core = group // 2, group % 2
    xx, yy, zhi = me // 8, (me // 2) % 4, me % 2

    def far(dz, r):
        dx, dy, dh = r // 8, (r // 2) % 4, r % 2
        e = (((xx + dx) % 4) * 4 + (yy + dy) % 4) * 2 + (zhi + dh) % 2
        return (zlo + dz) % 2, e

    def near(k):
        dz, dc, dh = k // 4, (k // 2) % 2, k % 2
        zl, c, zh = (zlo + dz) % 2, (core + dc) % 2, (zhi + dh) % 2
        return zl, c, zh, (zh * 2 + zl) * 2 + c

    def remote(src, dst, send, recv, device):
        return pltpu.make_async_remote_copy(
            src_ref=src, dst_ref=dst, send_sem=send, recv_sem=recv, device_id=device, device_id_type=MESH
        )

    def arrived(ref, sem):
        pltpu.make_async_copy(ref, ref, sem).wait()

    partner = (zlo * 2 + 1 - core, me)

    loads = [
        pltpu.make_async_copy(src, dst, in_sem.at[k])
        for k, (src, dst) in enumerate(((wd_hbm, wd), (x_hbm, x), (g_hbm, g), (win_hbm, win), (wout_hbm, wout)))
    ]
    loads[0].start()
    loads[1].start()

    barrier = pltpu.get_barrier_semaphore()

    def greet(k, _):
        zl, e = far(k // N, k % N)
        pl.semaphore_signal(barrier, inc=1, device_id=(zl * 2 + core, e), device_id_type=MESH)
        return 0

    lax.fori_loop(1, 2 * N, greet, 0)
    pl.semaphore_signal(barrier, inc=1, device_id=partner, device_id_type=MESH)
    for dz, dh in ((0, 1), (1, 0), (1, 1)):
        e = (xx * 4 + yy) * 2 + (zhi + dh) % 2
        pl.semaphore_signal(
            barrier, inc=1, device_id=(((zlo + dz) % 2) * 2 + 1 - core, e), device_id_type=MESH
        )

    def image(i):
        return pl.ds(i * TOK, TOK)

    def pick(i):
        row = lax.broadcasted_iota(jnp.int32, (EXP, ROWS), 0)
        col = lax.broadcasted_iota(jnp.int32, (EXP, ROWS), 1)
        return jnp.where(col == row * IMG + i, 1.0, 0.0).astype(BF16)

    def spread(low, out):
        for i in range(IMG):
            out[:, image(i)] = dot(pick(i), low[:, image(i)], TN).astype(BF16)

    loads[0].wait()
    loads[1].wait()
    for load in loads[2:]:
        load.start()
    for i in range(IMG):
        scores = dot(wd[...], x[image(i), :], NT)
        com[:, image(i)] = scores
        up = jnp.exp(scores - jnp.max(scores, axis=1, keepdims=True))
        d = up / jnp.sum(up, axis=1, keepdims=True)
        dis[:, image(i)] = d
        dis_low[:, image(i)] = d.astype(BF16)
    spread(dis_low, spread_low)
    send1[...] = pack_rows(dot(spread_low[...], x[...]))
    pl.semaphore_wait(barrier, 2 * N - 1 + 4)

    def dispatch(send, rows, which, first, last):
        def one(k, _):
            zl, e = far(k // N, k % N)
            remote(
                send.at[e], rows.at[core * 2 * N + zlo * N + me], s_sem.at[which, k // N], d_sem.at[which, zlo],
                (zl * 2 + core, e),
            ).start()
            return 0

        if first == 1:
            pltpu.make_async_copy(send.at[me], rows.at[core * 2 * N + zlo * N + me], d_sem.at[which, zlo]).start()
        lax.fori_loop(first, last, one, 0)

    def left(which, dz):
        arrived(r1.at[pl.ds(0, N - 1 + dz)], s_sem.at[which, dz])

    dispatch(send1, r1, 0, 1, 2 * N)
    for i in range(IMG):
        scores = com[:, image(i)]
        up = jnp.exp(scores - jnp.max(scores, axis=0, keepdims=True))
        c = up / jnp.sum(up, axis=0, keepdims=True)
        com[:, image(i)] = c
        com_low[:, image(i)] = c.astype(BF16)
    spread(com_low, spread_low)
    loads[2].wait()
    send2[...] = pack_rows(dot(spread_low[...], g[...]))
    left(0, 0)
    dispatch(send2, r2, 1, 1, N)
    outs = []

    def emit(src, dst, k):
        copy = pltpu.make_async_copy(src, dst, out_sem.at[k])
        copy.start()
        outs.append(copy)


    def quarter(c, dz):
        return pl.ds(c * 2 * N + ((zlo + dz) % 2) * N, N)

    def per_expert(rows, out, c, dz, at):
        base = c * 2 * N + ((zlo + dz) % 2) * N

        def step(s, _):
            first, second = split_experts(rows[pl.ds(base + s * 8, 8)].astype(F32))
            to = pl.ds(pl.multiple_of(at * 4 * N + s * 32, 32), 32)
            out[0, to, :] = first
            out[1, to, :] = second
            return 0

        lax.fori_loop(0, N // 8, step, 0)

    def forward(c, dz, at):
        per_expert(r1, e1, c, dz, at)
        to = pl.ds(pl.multiple_of(at * 4 * N, 4 * N), 4 * N)
        partial = []
        for ex in range(2):
            value, grad = gelu_pair(dot(e1[ex, to, :], win[ex]))
            slope[ex, to, :] = grad.astype(BF16)
            low = value.astype(BF16)
            act[ex, to, :] = low
            partial.append(dot(low, wout[ex]))
        p1[quarter(c, dz)] = join_experts(*partial)

    def backward(c, dz, at):
        per_expert(r2, e2, c, dz, at)
        to = pl.ds(pl.multiple_of(at * 4 * N, 4 * N), 4 * N)
        partial = []
        for ex in range(2):
            low = (dot(e2[ex, to, :], wout[ex], NT) * slope[ex, to, :].astype(F32)).astype(BF16)
            pre[ex, to, :] = low
            partial.append(dot(low, win[ex], NT))
        r1[quarter(c, dz)] = join_experts(*partial)

    def add_other(p, which, dz):
        arrived(pc.at[pl.ds(dz * N, N)], b_sem.at[which, dz])
        zl = (zlo + dz) % 2
        base = core * 2 * N + zl * N

        def add(s, _):
            at = pl.ds(base + s * 8, 8)
            p[at] = (p[at].astype(F32) + pc[pl.ds(dz * N + s * 8, 8)].astype(F32)).astype(BF16)
            return 0

        lax.fori_loop(0, N // 8, add, 0)

    def give_back(p, ret, which, dz):
        zl = (zlo + dz) % 2
        base = core * 2 * N + zl * N
        to = ret.at[zlo * N + me]

        def one(r, _):
            _, e = far(dz, r)
            remote(p.at[base + e], to, ssem.at[6 + which], ret_sem.at[which], (zl * 2 + core, e)).start()
            return 0

        if dz == 0:
            pltpu.make_async_copy(p.at[base + me], to, ret_sem.at[which]).start()
        lax.fori_loop(1 - dz, N, one, 0)

    def share(rows, which):
        for dz in range(2):
            block = rows.at[quarter(core, dz)]
            arrived(block, d_sem.at[which, (zlo + dz) % 2])
            remote(block, block, ssem.at[2 + which], c_sem.at[which, dz], partner).start()

    def experts(step, rows, p, which):
        def own(dz, _):
            step(core, dz, dz)
            return 0

        def other(dz, _):
            theirs = quarter(1 - core, dz)
            arrived(rows.at[theirs], c_sem.at[which, dz])
            step(1 - core, dz, 2 + dz)
            remote(
                p.at[theirs], pc.at[pl.ds(dz * N, N)], ssem.at[4 + which], b_sem.at[which, dz], partner
            ).start()
            return 0

        lax.fori_loop(0, 2, own, 0)
        lax.fori_loop(0, 2, other, 0)

    loads[3].wait()
    loads[4].wait()
    share(r1, 0)
    dispatch(send2, r2, 1, N, 2 * N)
    experts(forward, r1, p1, 0)
    add_other(p1, 0, 0)
    give_back(p1, ret1, 0, 0)
    add_other(p1, 0, 1)
    share(r2, 1)
    give_back(p1, ret1, 0, 1)
    arrived(r1.at[pl.ds(0, 2 * N)], ssem.at[2])
    experts(backward, r2, r1, 1)
    for dz in range(2):
        add_other(r1, 1, dz)
        give_back(r1, ret2, 1, dz)

    gwin_parts, gwout_parts = (win0, win1, win2, win3, win4), (wout0, wout1, wout2, wout3, wout4)
    stores = []
    for m in range(5):
        if m >= 2:
            for copy in stores[m - 2]:
                copy.wait()
        slot = m % 2
        cut, wide = pl.ds(m * 128, 128), pl.ds(m * 256, 256)
        for ex in range(2):
            (eo, sg)[slot][ex] = dot(act[ex, :, cut], e2[ex], TN).astype(BF16)
            gwin[slot, ex] = dot(e1[ex, :, wide], pre[ex], TN).astype(BF16)
        copies = [
            pltpu.make_async_copy(gwin.at[slot], gwin_parts[m], w_sem.at[2 * m]),
            pltpu.make_async_copy((eo, sg)[slot], gwout_parts[m], w_sem.at[2 * m + 1]),
        ]
        for copy in copies:
            copy.start()
        stores.append(copies)

    def returned(ret, which):
        arrived(ret, ret_sem.at[which])
        return unpack_rows(ret[pl.ds(0, N)].astype(F32) + ret[pl.ds(N, N)].astype(F32)).astype(BF16)

    rows = returned(ret1, 0)
    for copy in stores[3] + stores[4]:
        copy.wait()
    for i in range(IMG):
        slots = dot(pick(i), rows).astype(BF16)
        c = com[:, image(i)]
        dc = dot(slots, g[image(i), :], NT)
        com[:, image(i)] = c * (dc - jnp.sum(c * dc, axis=0, keepdims=True))
        g[image(i), :] = dot(com_low[:, image(i)], slots, TN).astype(BF16)
        emit(g.at[image(i)], (mix0, mix1, mix2, mix3)[i], i)

    rows = returned(ret2, 1)
    for i in range(IMG):
        slots = dot(pick(i), rows).astype(BF16)
        sg[i // 2, EXP * (i % 2) : EXP * (i % 2 + 1), :] = slots
        d = dis[:, image(i)]
        dd = dot(slots, x[image(i), :], NT)
        term = d * (dd - jnp.sum(d * dd, axis=1, keepdims=True))
        lgrad[:, image(i)] = (com[:, image(i)] + term).astype(BF16)
    gd[...] = pack_rows(dot(lgrad[...], x[...]))

    block = (zhi * 2 + zlo) * 2 + core

    def near_device(k):
        zl, c, zh, b = near(k)
        return (zl * 2 + c, (xx * 4 + yy) * 2 + zh), b

    for k in range(1, 8):
        device, b = near_device(k)
        remote(gd.at[b], ar_a.at[k], ssem.at[8], ar_sem.at[0], device).start()

    def image_grad(i):
        left = jnp.concatenate([lgrad[:, image(i)], dis_low[:, image(i)]], axis=0)
        right = jnp.concatenate([wd[...], sg[i // 2, EXP * (i % 2) : EXP * (i % 2 + 1), :]], axis=0)
        x[image(i), :] = dot(left, right, TN).astype(BF16)
        emit(x.at[image(i)], (grad0, grad1, grad2, grad3)[i], 4 + i)

    image_grad(0)
    arrived(ar_a.at[pl.ds(1, 7)], ar_sem.at[0])
    total = gd[block].astype(F32)
    for k in range(1, 8):
        total += ar_a[k].astype(F32)
    ar_x[xx] = total.astype(BF16)
    for k in range(1, 4):
        remote(
            ar_x.at[xx], ar_x.at[xx], ssem.at[9], ar_sem.at[1], (group, (((xx + k) % 4) * 4 + yy) * 2 + zhi)
        ).start()

    def sum4(ref):
        return ((ref[0].astype(F32) + ref[1].astype(F32)) + (ref[2].astype(F32) + ref[3].astype(F32))).astype(BF16)

    image_grad(1)
    arrived(ar_x.at[pl.ds(0, 3)], ar_sem.at[1])
    ar_y[yy] = sum4(ar_x)
    for k in range(1, 4):
        remote(
            ar_y.at[yy], ar_y.at[yy], ssem.at[10], ar_sem.at[2], (group, (xx * 4 + (yy + k) % 4) * 2 + zhi)
        ).start()
    image_grad(2)
    arrived(ar_y.at[pl.ds(0, 3)], ar_sem.at[2])
    gdo[block] = sum4(ar_y)
    for k in range(1, 8):
        device, _ = near_device(k)
        remote(gdo.at[block], gdo.at[block], ssem.at[11], ar_sem.at[3], device).start()
    image_grad(3)
    arrived(gdo.at[pl.ds(0, 7)], ar_sem.at[3])
    emit(gdo, gd_out, 8)

    for which in range(2):
        left(which, 1)
        if which == 1:
            left(which, 0)
        if which == 1:
            arrived(r1.at[pl.ds(0, 2 * N)], ssem.at[2 + which])
        arrived(r1.at[pl.ds(0, 2 * N)], ssem.at[4 + which])
        arrived(r1.at[pl.ds(0, 2 * N - 1)], ssem.at[6 + which])
    arrived(gd.at[pl.ds(0, 7)], ssem.at[8])
    arrived(ar_x.at[pl.ds(0, 3)], ssem.at[9])
    arrived(ar_y.at[pl.ds(0, 3)], ssem.at[10])
    arrived(gd.at[pl.ds(0, 7)], ssem.at[11])
    for copy in outs:
        copy.wait()


def finish(*refs):
    parts, (gd_in, mixed, gimg, gsum, gwin, gwout), (gd, wide, out_sem) = refs[:18], refs[18:24], refs[24:]
    load = pltpu.make_async_copy(gd_in, gd, out_sem.at[18])
    load.start()
    places = [mixed.at[pl.ds(i * TOK, TOK)] for i in range(IMG)] + [gimg.at[pl.ds(i * TOK, TOK)] for i in range(IMG)]
    places += [gwin.at[:, pl.ds(m * 256, 256)] for m in range(5)] + [gwout.at[:, pl.ds(m * 128, 128)] for m in range(5)]
    copies = [pltpu.make_async_copy(part, place, out_sem.at[k]) for k, (part, place) in enumerate(zip(parts, places))]
    for copy in copies:
        copy.start()
    load.wait()
    wide[...] = unpack_rows(gd[...].astype(F32))
    copies.append(pltpu.make_async_copy(wide, gsum, out_sem.at[19]))
    copies[-1].start()
    for copy in copies:
        copy.wait()


def per_device(images, dispatch_weight, weight_in, weight_out, out_grad):
    vmem = pltpu.VMEM
    message = (16, HALF)
    scratch = [
        vmem((T, D), BF16), vmem((EXP, D), BF16), vmem((2, D, HIDQ), BF16), vmem((2, HIDQ, D), BF16), vmem((T, D), BF16),
        vmem((N, *message), BF16), vmem((N, *message), BF16),
        vmem((4 * N, *message), BF16), vmem((4 * N, *message), BF16),
        vmem((2, 16 * N, D), BF16), vmem((2, 16 * N, D), BF16),
        vmem((2, 16 * N, HIDQ), BF16), vmem((2, 16 * N, HIDQ), BF16), vmem((2, 16 * N, HIDQ), BF16),
        vmem((4 * N, *message), BF16),
        vmem((2 * N, *message), BF16),
        vmem((2 * N, *message), BF16), vmem((2 * N, *message), BF16),
        vmem((EXP, T), F32), vmem((EXP, T), F32), vmem((EXP, T), BF16), vmem((EXP, T), BF16),
        vmem((ROWS, T), BF16),
        vmem((EXP, T), BF16), vmem((2, 2 * EXP, D), BF16), vmem((2, 2 * EXP, D), BF16),
        vmem((2, 2, 256, HIDQ), BF16),
        vmem((8, *message), BF16), vmem((8, *message), BF16), vmem((4, *message), BF16), vmem((4, *message), BF16),
        vmem((8, *message), BF16),
        pltpu.SemaphoreType.DMA((5,)), pltpu.SemaphoreType.DMA((9,)), pltpu.SemaphoreType.DMA((10,)), pltpu.SemaphoreType.DMA((2, 2)),
        pltpu.SemaphoreType.DMA((12,)),
        pltpu.SemaphoreType.DMA((2, 2)), pltpu.SemaphoreType.DMA((2, 2)), pltpu.SemaphoreType.DMA((2, 2)),
        pltpu.SemaphoreType.DMA((2,)), pltpu.SemaphoreType.DMA((4,)),
    ]
    anywhere = pl.BlockSpec(memory_space=pl.ANY)
    tokens = jax.ShapeDtypeStruct((T, D), BF16)
    first, second = jax.ShapeDtypeStruct((2, D, HIDQ), BF16), jax.ShapeDtypeStruct((2, HIDQ, D), BF16)
    wd = dispatch_weight.T
    gd_shape = jax.ShapeDtypeStruct((8, *message), BF16)
    parts = pl.pallas_call(
        kernel,
        out_shape=(jax.ShapeDtypeStruct((TOK, D), BF16),) * 8
        + (jax.ShapeDtypeStruct((2, 256, HIDQ), BF16),) * 5
        + (jax.ShapeDtypeStruct((2, 128, D), BF16),) * 5
        + (gd_shape,),
        in_specs=[anywhere] * 5,
        out_specs=[anywhere] * 19,
        scratch_shapes=scratch,
        compiler_params=pltpu.CompilerParams(
            collective_id=0, has_side_effects=True, vmem_limit_bytes=LIMIT * 2**20
        ),
    )(images.reshape(T, D), wd, weight_in, weight_out, out_grad.reshape(T, D))
    mixed, gimg, gd, gwin, gwout = pl.pallas_call(
        finish,
        out_shape=(tokens, tokens, jax.ShapeDtypeStruct((EXP, D), F32), first, second),
        in_specs=[anywhere] * 19,
        out_specs=[anywhere] * 5,
        scratch_shapes=[vmem((8, *message), BF16), vmem((EXP, D), F32), pltpu.SemaphoreType.DMA((20,))],
        compiler_params=pltpu.CompilerParams(vmem_limit_bytes=12 * 2**20),
    )(*parts)
    return mixed.reshape(IMG, TOK, D), gimg.reshape(IMG, TOK, D), gd.T, gwin, gwout


def solution(mesh):
    tokens = P(("group", "expert"), None, None)
    first, second = P("expert", None, "group"), P("expert", "group", None)
    return jax.shard_map(
        per_device,
        mesh=mesh,
        in_specs=(tokens, P(), first, second, tokens),
        out_specs=(tokens, tokens, P(), first, second),
        check_vma=False,
    )
```
